32 devices in a mesh: grp: 4 (over z), blk: 8 (over y, x, core).
Axes of the slice: x: 2, y: 2, z: 4, core: 2. Of those that a mesh axis runs over, the one named last changes fastest.
Arguments:
- slab: bfloat16 [16, 2048, 2048], P('grp', 'blk'), may hold values from -0.59765625 to 0.59765625
- block_mask: int32 [4, 64, 64], P('grp', 'blk'), may hold values 0 or 1
- orbitals: bfloat16 [2048, 1024], P('blk'), may hold values from -0.125 to 0.125
- margin: bfloat16 [2048, 2048], P('blk', 'grp'), as said below
- env_flag: int32 [1024], replicated, may hold values from 0 to 1
Outputs:
- projected: float32 [2048, 2048], P('blk', 'grp')
The draws below stay inside these ranges and needn't reach their ends.
Inputs may be any that keep to these rules, and one draw needn't show every extreme that they name: margin is symmetric positive definite with unit diagonal.
All inputs are finite; a program needn't handle non-finite values. No bound on the sum of `block_mask` on one device may be relied on, other than what follows from the above.
Results may differ from the reference program's by a relative error of at most 0.003.
Values may be sent and summed in bfloat16 or wider, within the bound.
A program may use at most 128 MiB of HBM per device.

```python
import jax
import jax.numpy as jnp
from jax import lax

AUX_DEV = 4
OCC = 1024
ATILE = 32
NAO = 2048
AUX = 16
NAOB = 64
N_GRP = 4


def draw_margin(key, part):
    noise = jax.random.normal(key, (NAO, NAO), jnp.float32)
    sym = (noise + noise.T) * (0.25 / NAO ** 0.5)
    eye = jnp.eye(NAO, dtype=jnp.float32)
    return (eye + sym * (1.0 - eye)).astype(jnp.bfloat16)


def set_ends(result, rng, low, top_value):
    dims = result.shape
    place = [jax.random.randint(jax.random.fold_in(rng, axis), (), 0, dims[axis]) for axis in range(len(dims))]
    result = result.at[tuple(place)].set(low)
    longest = dims.index(max(dims))
    place[longest] = (place[longest] + 1) % dims[longest]
    return result.at[tuple(place)].set(top_value)


def block_levels(rng, extent, shards, smallest, high):
    gain = 1.0
    for axis_at, shards_of in shards:
        steps = jax.random.uniform(jax.random.fold_in(jax.random.fold_in(rng, 6), axis_at), (shards_of,), jnp.float32, smallest / len(shards), high / len(shards))
        gain = gain * jnp.repeat(jnp.exp(steps), extent[axis_at] // shards_of).reshape((-1,) + (1,) * (len(extent) - 1 - axis_at))
    return gain


def bell_draw(stream_key, extent, deviation, most, pieces=(), held_as=jnp.bfloat16):
    drawn = deviation * jax.random.normal(stream_key, extent, jnp.float32)
    if pieces:
        drawn = drawn * block_levels(stream_key, extent, pieces, -0.22, 0.18)
    return jnp.clip(drawn, -most, most).astype(held_as)


def setup_inputs(seed: int = 0) -> dict:
    key_of = jax.random.split(jax.random.key(seed), 6)
    return {
        "slab": bell_draw(key_of[0], (AUX, NAO, NAO), 0.1, 0.59765625, ((0, 4), (1, 8))),
        "block_mask": set_ends((jax.random.randint(key_of[1], (N_GRP, NAOB, NAOB), 0, 5) < 3).astype(jnp.int32), jax.random.fold_in(key_of[1], 1), 0, 1),
        "orbitals": bell_draw(key_of[2], (NAO, OCC), NAO ** -0.5, 0.125, ((0, 8),)),
        "margin": draw_margin(jax.random.fold_in(key_of[5], 71), 0),
        "env_flag": set_ends(jax.random.randint(key_of[4], (OCC,), 0, 2), jax.random.fold_in(key_of[4], 1), 0, 1).astype(jnp.int32),
    }


def reference(slab, block_mask, orbitals, margin, env_flag):
    def transform(index):
        tiles = block_mask[index // AUX_DEV]
        keep_full = jnp.repeat(jnp.repeat(tiles, ATILE, axis=0), ATILE, axis=1).astype(jnp.bfloat16)
        masked = slab[index] * keep_full
        return jnp.dot(masked, orbitals, preferred_element_type=jnp.float32).astype(jnp.bfloat16)

    half = lax.map(transform, jnp.arange(AUX, dtype=jnp.int32))

    def accumulate(total, piece):
        return total + jnp.dot(piece, piece.T, preferred_element_type=jnp.float32), None

    exchange, unused = lax.scan(accumulate, jnp.zeros((NAO, NAO), jnp.float32), half)
    env_orbitals = orbitals * env_flag.astype(jnp.bfloat16)[None, :]
    exchange_bf = exchange.astype(jnp.bfloat16)
    left_env = jnp.dot(env_orbitals.T, exchange_bf, preferred_element_type=jnp.float32).astype(jnp.bfloat16)
    env_margin = jnp.dot(env_orbitals.T, margin, preferred_element_type=jnp.float32).astype(jnp.bfloat16)
    right_env = jnp.dot(exchange_bf, env_orbitals, preferred_element_type=jnp.float32).astype(jnp.bfloat16)
    margin_env = jnp.dot(margin, env_orbitals, preferred_element_type=jnp.float32).astype(jnp.bfloat16)
    first = jnp.dot(margin_env, left_env, preferred_element_type=jnp.float32)
    second = jnp.dot(right_env, env_margin, preferred_element_type=jnp.float32)
    return exchange - first - second
```

```python
import jax
import jax.numpy as jnp
from jax import lax
from jax.sharding import PartitionSpec as P

ATILE = 32


def dot32(left, right, dims):
    return lax.dot_general(left, right, (dims, ((), ())), preferred_element_type=jnp.float32)


def pair_block(half, other):
    return jnp.einsum("pmi,pni->mn", half, other, preferred_element_type=jnp.float32)


def on_device(slab, block_mask, orbitals, margin, env_flag):
    bf16 = jnp.bfloat16
    aux_dev, ao_dev, nao = slab.shape
    keep_tile = jnp.repeat(jnp.repeat(block_mask[0], ATILE, axis=0), ATILE, axis=1).astype(bf16)
    masked = slab * keep_tile[None, :, :]
    whole_c = lax.all_gather(orbitals, "blk", axis=0, tiled=True)
    margin_rows = lax.all_gather(margin, "grp", axis=1, tiled=True)
    margin_cols = lax.all_gather(margin, "blk", axis=0, tiled=True)
    occ = whole_c.shape[1]
    half = jnp.dot(
        masked.reshape(aux_dev * ao_dev, nao), whole_c, preferred_element_type=jnp.float32
    )
    half = half.astype(bf16).reshape(aux_dev, ao_dev, occ)
    rows_k = pair_block(half, lax.all_gather(half, "blk", axis=1, tiled=True))
    env = whole_c * env_flag.astype(bf16)[None, :]
    t_rows = dot32(dot32(margin_rows, env, ((1,), (0,))).astype(bf16), env, ((1,), (1,))).astype(bf16)
    t_cols = dot32(dot32(margin_cols, env, ((0,), (0,))).astype(bf16), env, ((1,), (1,))).astype(bf16)
    k_tile = lax.psum_scatter(rows_k, "grp", scatter_dimension=1, tiled=True)
    k_bf = k_tile.astype(bf16)
    k_cols = lax.all_gather(k_bf, "blk", axis=0, tiled=True)
    k_rows = lax.all_gather(k_bf, "grp", axis=1, tiled=True)
    first = dot32(t_rows, k_cols, ((1,), (0,)))
    second = dot32(k_rows, t_cols, ((1,), (1,)))
    return k_tile - first - second


def solution(mesh):
    placed = (P("grp", "blk", None), P("grp", "blk", None), P("blk", None), P("blk", "grp"), P())
    return jax.shard_map(
        on_device, mesh=mesh, in_specs=placed, out_specs=P("blk", "grp"), check_vma=False
    )
```

```python
import functools

import jax
import jax.numpy as jnp
from jax import lax
from jax.experimental import pallas as pl
from jax.experimental.pallas import tpu as pltpu
from jax.sharding import PartitionSpec as P

ATILE = 32
MESH = pl.DeviceIdType.MESH
BF16 = jnp.bfloat16
F32 = jnp.float32
OF_C, OF_H, OF_K, OF_S = range(4)


def dot_nn(left, right):
    return lax.dot_general(left, right, (((1,), (0,)), ((), ())), preferred_element_type=F32)


def dot_nt(left, right):
    return lax.dot_general(left, right, (((1,), (1,)), ((), ())), preferred_element_type=F32)


def dot_tn(left, right):
    return lax.dot_general(left, right, (((0,), (0,)), ((), ())), preferred_element_type=F32)


def flipped(index, step):
    bit = 1
    while bit <= step:
        if step & bit:
            index = index + bit - 2 * bit * lax.rem(lax.div(index, bit), 2)
        bit *= 2
    return index


def kernel(
    n_grp, n_blk,
    keep_ref, env_ref, orb_ref, margin_ref, slab_hbm, out_ref,
    slab, c_all, acc, h_own, h_buf, zt_send, zt_recv, k_recv,
    k_cols, k_rows, s_cols, s_rows, mid,
    load_sem, dir_s, dir_r, fwd_s, fwd_r, zt_s, zt_r, sum_s, sum_r, kz_s, kz_r, sz_s, sz_r,
):
    z = lax.axis_index("grp")
    b = lax.axis_index("blk")
    n_chip = n_blk // 2
    chip, core = lax.div(b, 2), lax.rem(b, 2)
    sib = chip * 2 + 1 - core
    aux, rows, nao = slab.shape
    half_aux = aux // 2
    width = 2 * rows
    steps = range(1, n_chip)
    sent = []

    load = pltpu.make_async_copy(slab_hbm, slab, load_sem)
    load.start()

    barrier = pltpu.get_barrier_semaphore()
    for s in range(1, n_blk):
        pl.semaphore_signal(barrier, inc=1, device_id=(z, lax.rem(b + s, n_blk)), device_id_type=MESH)
    for s in range(1, n_grp):
        pl.semaphore_signal(barrier, inc=1, device_id=(lax.rem(z + s, n_grp), b), device_id_type=MESH)
    pl.semaphore_wait(barrier, n_blk + n_grp - 2)

    def remote(src, dst, send_sem, recv_sem, to):
        return pltpu.make_async_remote_copy(
            src_ref=src, dst_ref=dst, send_sem=send_sem, recv_sem=recv_sem,
            device_id=to, device_id_type=MESH,
        )

    def send(src, dst, send_sem, recv_sem, to):
        copy = remote(src, dst, send_sem, recv_sem, to)
        copy.start()
        sent.append(copy)

    def arrived(dst, send_sem, recv_sem):
        remote(dst, dst, send_sem, recv_sem, (z, sib)).wait_recv()

    def to_chip(kind, s, src, dst):
        send(src, dst, dir_s.at[kind, s], dir_r.at[kind, s], (z, flipped(chip, s) * 2 + core))

    def from_chip(kind, s, dst):
        arrived(dst, dir_s.at[kind, s], dir_r.at[kind, s])

    def to_sib(kind, s, ref):
        send(ref, ref, fwd_s.at[kind, s], fwd_r.at[kind, s], (z, sib))

    def from_sib(kind, s, dst):
        arrived(dst, fwd_s.at[kind, s], fwd_r.at[kind, s])

    per_acc = acc.shape[2] // rows

    def k_block(j):
        start = pl.multiple_of(lax.rem(j, per_acc) * rows, rows)
        return acc.at[lax.div(j, per_acc), :, pl.ds(start, rows)]

    def t_row(j):
        return slab.at[2, :, pl.ds(pl.multiple_of(j * rows, rows), rows)]

    def t_col(j):
        start = pl.multiple_of(lax.rem(j, n_grp) * width, width)
        return slab.at[lax.div(j, n_grp), :, pl.ds(start, width)]

    def k_send(c):
        return slab.at[3, :, pl.ds(pl.multiple_of(c * width, width), width)]

    def c_block(index):
        return c_all.at[pl.ds(pl.multiple_of(index * rows, rows), rows)]

    c_block(b)[...] = orb_ref[...]
    to_sib(OF_C, 0, c_block(b))
    for s in steps:
        to_chip(OF_C, s, c_block(b), c_block(b))
    s_rows[z] = margin_ref[...]
    s_cols[b] = margin_ref[...]
    for s in range(1, n_grp):
        send(s_rows.at[z], s_rows.at[z], sz_s.at[s], sz_r.at[s], (flipped(z, s), b))

    load.wait()
    tiles = rows // ATILE
    for t in range(tiles):
        keep = jnp.broadcast_to(keep_ref[t : t + 1, :], (ATILE, nao)).astype(BF16)

        @pl.loop(0, aux)
        def _(p):
            slab[p, t * ATILE : (t + 1) * ATILE, :] = slab[p, t * ATILE : (t + 1) * ATILE, :] * keep

    def half_part(p, c):
        start = pl.multiple_of(c * width, width)
        return dot_nn(slab[p, :, pl.ds(start, width)], c_all[pl.ds(start, width), :])

    from_sib(OF_C, 0, c_block(sib))

    for s in steps:
        c_new, c_old = flipped(chip, s), flipped(chip, s - 1)
        from_chip(OF_C, s, c_block(c_new * 2 + core))
        to_sib(OF_C, s, c_block(c_new * 2 + core))

        @pl.loop(0, aux)
        def _(p):
            part = half_part(p, c_old)
            acc[p] = part if s == 1 else acc[p] + part

        from_sib(OF_C, s, c_block(c_new * 2 + 1 - core))

    c_last = flipped(chip, n_chip - 1)

    @pl.loop(0, aux)
    def _(p):
        h_own[p] = (acc[p] + half_part(p, c_last)).astype(BF16)

    def h_slot(c, a):
        return h_buf.at[pl.ds(c * aux + a * half_aux, half_aux)]

    def upper(s):
        top = 1 << (s.bit_length() - 1)
        return lax.rem(lax.div(chip, top), 2)

    for s in steps:
        first = half_aux * (1 - upper(s))
        to_chip(OF_H, s, h_own.at[pl.ds(first, half_aux)], h_slot(chip, core))
    own_slot = h_buf.at[pl.ds(chip * aux, aux)]
    send(h_own, own_slot, fwd_s.at[OF_H, 0], fwd_r.at[OF_H, 0], (z, sib))

    def pair(own_first, other, other_first, count):
        def add(p, total):
            return total + dot_nt(h_own[own_first + p], other[other_first + p])

        return lax.fori_loop(0, count, add, jnp.zeros((rows, rows), F32))

    k_block(b)[...] = pair(0, h_own, 0, aux)

    for s in range(1, n_grp):
        arrived(s_rows.at[flipped(z, s)], sz_s.at[s], sz_r.at[s])
    mid[:rows] = jnp.zeros((rows, mid.shape[1]), F32)

    @pl.loop(0, n_grp)
    def _(g):
        start = pl.multiple_of(g * width, width)
        mid[:rows] += dot_nn(s_rows[g], c_all[pl.ds(start, width), :])

    m_rows = (mid[:rows] * env_ref[...]).astype(BF16)

    @pl.loop(0, n_blk)
    def _(j):
        t_row(j)[...] = dot_nt(m_rows, c_block(j)[...]).astype(BF16)

    from_sib(OF_H, 0, own_slot)
    k_block(sib)[...] = pair(0, h_buf, chip * aux, aux)

    def sum_copy(c):
        return remote(k_send(c), k_recv.at[z], sum_s.at[c], sum_r.at[z], (c, b))

    def finish_chunk(c):
        for a in range(2):
            at = pl.multiple_of(c * width + a * rows, rows)
            slab[3, :, pl.ds(at, rows)] = k_block(2 * c + a)[...].astype(BF16)

        @pl.when(c != z)
        def _():
            sum_copy(c).start()

    finish_chunk(chip)

    def exchange_block(s, a):
        c = flipped(chip, s)
        other = 2 * c + a
        block = pair(half_aux * upper(s), h_buf, c * aux + a * half_aux, half_aux)
        k_block(other)[...] = block
        zt_send[other] = block.T.astype(BF16)
        send(zt_send.at[other], zt_recv.at[b], zt_s.at[2 * s + a], zt_r.at[2 * s + core], (z, other))

    def add_block(s):
        c = flipped(chip, s)
        for a in range(2):
            other = 2 * c + a
            arrived(zt_recv.at[other], zt_s.at[2 * s + a], zt_r.at[2 * s + a])
            k_block(other)[...] += zt_recv[other].astype(F32)
        finish_chunk(c)

    for s in steps:
        c = flipped(chip, s)
        from_chip(OF_H, s, h_slot(c, core))
        to_sib(OF_H, s, h_slot(c, core))
        exchange_block(s, core)
        from_sib(OF_H, s, h_slot(c, 1 - core))
        exchange_block(s, 1 - core)
        if s > 1:
            add_block(s - 1)
    to_sib(OF_S, 0, s_cols.at[b])
    for s in steps:
        to_chip(OF_S, s, s_cols.at[b], s_cols.at[b])
    add_block(n_chip - 1)

    from_sib(OF_S, 0, s_cols.at[sib])
    for s in steps:
        c = flipped(chip, s)
        from_chip(OF_S, s, s_cols.at[2 * c + core])
        to_sib(OF_S, s, s_cols.at[2 * c + core])
    for s in steps:
        from_sib(OF_S, s, s_cols.at[2 * flipped(chip, s) + 1 - core])
    mid[...] = jnp.zeros(mid.shape, F32)

    @pl.loop(0, n_blk)
    def _(j):
        mid[...] += dot_tn(s_cols[j], c_block(j)[...])

    m_cols = (mid[...] * env_ref[...]).astype(BF16)

    @pl.loop(0, n_blk)
    def _(j):
        t_col(j)[...] = dot_nt(c_block(j)[...], m_cols).astype(BF16)

    k_tile = jnp.concatenate([k_block(2 * z)[...], k_block(2 * z + 1)[...]], axis=1)
    for s in range(1, n_grp):
        other = flipped(z, s)
        arrived(k_recv.at[other], sum_s.at[other], sum_r.at[other])
        k_tile = k_tile + k_recv[other].astype(F32)
    k_bf = k_tile.astype(BF16)
    out_ref[...] = k_tile
    k_cols[b] = k_bf
    k_rows[z] = k_bf
    for s in range(1, n_grp):
        send(k_rows.at[z], k_rows.at[z], kz_s.at[s], kz_r.at[s], (flipped(z, s), b))
    to_sib(OF_K, 0, k_cols.at[b])
    for s in steps:
        to_chip(OF_K, s, k_cols.at[b], k_cols.at[b])

    def take_first(j):
        out_ref[...] -= dot_nn(t_row(j)[...], k_cols[j])

    def take_second(g):
        out_ref[...] -= dot_nn(k_rows[g, :, :rows], t_col(2 * g)[...])
        out_ref[...] -= dot_nn(k_rows[g, :, rows:], t_col(2 * g + 1)[...])

    take_first(b)
    take_second(z)
    from_sib(OF_K, 0, k_cols.at[sib])
    take_first(sib)
    for s in steps:
        c = flipped(chip, s)
        from_chip(OF_K, s, k_cols.at[2 * c + core])
        to_sib(OF_K, s, k_cols.at[2 * c + core])
        take_first(2 * c + core)
    for s in steps:
        other = 2 * flipped(chip, s) + 1 - core
        from_sib(OF_K, s, k_cols.at[other])
        take_first(other)
    for s in range(1, n_grp):
        other = flipped(z, s)
        arrived(k_rows.at[other], kz_s.at[s], kz_r.at[s])
        take_second(other)

    for copy in sent:
        copy.wait_send()
    for s in range(n_chip):
        c = flipped(chip, s)

        @pl.when(c != z)
        def _():
            sum_copy(c).wait_send()


def on_device(n_grp, n_blk, slab, block_mask, orbitals, margin, env_flag):
    aux, rows, nao = slab.shape
    occ = orbitals.shape[1]
    width = margin.shape[1]
    n_chip = n_blk // 2
    assert width == 2 * rows and n_chip == n_grp and aux == 4
    keep = jnp.repeat(block_mask[0], ATILE, axis=1).astype(F32)
    env = env_flag.astype(F32)[None, :]
    vmem = pl.BlockSpec(memory_space=pltpu.VMEM)
    dma = pltpu.SemaphoreType.DMA
    return pl.pallas_call(
        functools.partial(kernel, n_grp, n_blk),
        out_shape=jax.ShapeDtypeStruct((rows, width), F32),
        in_specs=[vmem] * 4 + [pl.BlockSpec(memory_space=pl.ANY)],
        out_specs=vmem,
        scratch_shapes=[
            pltpu.VMEM((aux, rows, nao), BF16),
            pltpu.VMEM((nao, occ), BF16),
            pltpu.VMEM((aux, rows, occ), F32),
            pltpu.VMEM((aux, rows, occ), BF16),
            pltpu.VMEM((n_chip * aux, rows, occ), BF16),
            pltpu.VMEM((n_blk, rows, rows), BF16),
            pltpu.VMEM((n_blk, rows, rows), BF16),
            pltpu.VMEM((n_grp, rows, width), BF16),
            pltpu.VMEM((n_blk, rows, width), BF16),
            pltpu.VMEM((n_grp, rows, width), BF16),
            pltpu.VMEM((n_blk, rows, width), BF16),
            pltpu.VMEM((n_grp, rows, width), BF16),
            pltpu.VMEM((width, occ), F32),
            dma(()),
            dma((4, n_chip)), dma((4, n_chip)), dma((4, n_chip)), dma((4, n_chip)),
            dma((2 * n_chip,)), dma((2 * n_chip,)),
            dma((n_grp,)), dma((n_grp,)), dma((n_grp,)), dma((n_grp,)), dma((n_grp,)), dma((n_grp,)),
        ],
        compiler_params=pltpu.CompilerParams(
            collective_id=0, has_side_effects=True, vmem_limit_bytes=63 * 2**20
        ),
    )(keep, env, orbitals, margin, slab)


def solution(mesh):
    placed = (P("grp", "blk", None), P("grp", "blk", None), P("blk", None), P("blk", "grp"), P())
    return jax.shard_map(
        functools.partial(on_device, mesh.shape["grp"], mesh.shape["blk"]),
        mesh=mesh, in_specs=placed, out_specs=P("blk", "grp"), check_vma=False,
    )
```

```python
import functools

import jax
import jax.numpy as jnp
from jax import lax
from jax.experimental import pallas as pl
from jax.experimental.pallas import tpu as pltpu
from jax.sharding import PartitionSpec as P

ATILE = 32
MESH = pl.DeviceIdType.MESH
BF16 = jnp.bfloat16
F32 = jnp.float32
OF_C, OF_H, OF_K, OF_S = range(4)


def dot_nn(left, right):
    return lax.dot_general(left, right, (((1,), (0,)), ((), ())), preferred_element_type=F32)


def dot_nt(left, right):
    return lax.dot_general(left, right, (((1,), (1,)), ((), ())), preferred_element_type=F32)


def dot_tn(left, right):
    return lax.dot_general(left, right, (((0,), (0,)), ((), ())), preferred_element_type=F32)


def flipped(index, step):
    bit = 1
    while bit <= step:
        if step & bit:
            index = index + bit - 2 * bit * lax.rem(lax.div(index, bit), 2)
        bit *= 2
    return index


def kernel(
    n_grp, n_blk,
    mask_ref, env_ref, orb_ref, margin_ref, slab_hbm, out_ref,
    slab, c_all, acc, h_own, h_buf, zt_send, zt_recv, k_recv,
    k_cols, k_rows, s_cols, s_rows, mid,
    load_sem, dir_s, dir_r, fwd_s, fwd_r, zt_s, zt_r, sum_s, sum_r, kz_up, kz_down, kz_r, sz_s, sz_r,
):
    z = lax.axis_index("grp")
    b = lax.axis_index("blk")
    n_chip = n_blk // 2
    chip, core = lax.div(b, 2), lax.rem(b, 2)
    sib = chip * 2 + 1 - core
    aux, rows, nao = slab.shape
    half_aux = aux // 2
    width = 2 * rows
    steps = range(1, n_chip)
    two_hop = n_chip == 4
    bit1 = lax.div(chip, 2)
    parity = lax.rem(lax.rem(chip, 2) + bit1, 2)
    sent = []

    load = pltpu.make_async_copy(slab_hbm, slab, load_sem)
    load.start()

    barrier = pltpu.get_barrier_semaphore()
    for s in range(1, n_blk):
        pl.semaphore_signal(barrier, inc=1, device_id=(z, lax.rem(b + s, n_blk)), device_id_type=MESH)
    for s in range(1, n_grp):
        pl.semaphore_signal(barrier, inc=1, device_id=(lax.rem(z + s, n_grp), b), device_id_type=MESH)
    pl.semaphore_wait(barrier, n_blk + n_grp - 2)

    def remote(src, dst, send_sem, recv_sem, to):
        return pltpu.make_async_remote_copy(
            src_ref=src, dst_ref=dst, send_sem=send_sem, recv_sem=recv_sem,
            device_id=to, device_id_type=MESH,
        )

    def send(src, dst, send_sem, recv_sem, to):
        copy = remote(src, dst, send_sem, recv_sem, to)
        copy.start()
        sent.append(copy)

    def arrived(dst, send_sem, recv_sem):
        remote(dst, dst, send_sem, recv_sem, (z, sib)).wait_recv()

    def to_chip(kind, s, src, dst, i=0, via=None):
        to = (z, flipped(chip, via or s) * 2 + core)
        send(src, dst, dir_s.at[kind, s, i], dir_r.at[kind, s, i], to)

    def from_chip(kind, s, dst, i=0):
        arrived(dst, dir_s.at[kind, s, i], dir_r.at[kind, s, i])

    def to_sib(kind, s, ref, i=0):
        send(ref, ref, fwd_s.at[kind, s, i], fwd_r.at[kind, s, i], (z, sib))

    def from_sib(kind, s, dst, i=0):
        arrived(dst, fwd_s.at[kind, s, i], fwd_r.at[kind, s, i])

    per_acc = acc.shape[2] // rows

    def k_block(j):
        start = pl.multiple_of(lax.rem(j, per_acc) * rows, rows)
        return acc.at[lax.div(j, per_acc), :, pl.ds(start, rows)]

    def t_row(j):
        return slab.at[2, :, pl.ds(pl.multiple_of(j * rows, rows), rows)]

    def t_col(j):
        start = pl.multiple_of(lax.rem(j, n_grp) * width, width)
        return slab.at[lax.div(j, n_grp), :, pl.ds(start, width)]

    def k_send(c):
        return slab.at[3, :, pl.ds(pl.multiple_of(c * width, width), width)]

    def c_block(index):
        return c_all.at[pl.ds(pl.multiple_of(index * rows, rows), rows)]

    c_block(b)[...] = orb_ref[...]
    to_sib(OF_C, 0, c_block(b))

    def c_half(index, i):
        start = pl.multiple_of(index * rows + i * (rows // 2), rows // 2)
        return c_all.at[pl.ds(start, rows // 2)]

    if two_hop:
        for s, i in ((1, 0), (2, 1), (1, 1), (2, 0)):
            to_chip(OF_C, s, c_half(b, i), c_half(b, i), i)
    else:
        for s in steps:
            for i in range(2):
                to_chip(OF_C, s, c_half(b, i), c_half(b, i), i)
    s_rows[z] = margin_ref[...]
    s_cols[b] = margin_ref[...]
    for s in range(1, n_grp):
        send(s_rows.at[z], s_rows.at[z], sz_s.at[s], sz_r.at[s], (flipped(z, s), b))

    spread = lax.broadcasted_iota(jnp.int32, (nao // ATILE, nao), 1)
    tile = lax.broadcasted_iota(jnp.int32, (nao // ATILE, nao), 0) * ATILE
    spread = jnp.where((spread >= tile) & (spread < tile + ATILE), 1.0, 0.0).astype(BF16)
    keep_all = dot_nn(mask_ref[0].astype(F32).astype(BF16), spread)
    load.wait()
    for t in range(rows // ATILE):
        keep = jnp.broadcast_to(keep_all[t : t + 1, :], (ATILE, nao)).astype(BF16)

        @pl.loop(0, aux)
        def _(p):
            slab[p, t * ATILE : (t + 1) * ATILE, :] = slab[p, t * ATILE : (t + 1) * ATILE, :] * keep

    def half_part(p, c):
        start = pl.multiple_of(c * width, width)
        return dot_nn(slab[p, :, pl.ds(start, width)], c_all[pl.ds(start, width), :])

    from_sib(OF_C, 0, c_block(sib))

    def start_half(c, first):
        @pl.loop(0, aux)
        def _(p):
            part = half_part(p, c)
            acc[p] = part if first else acc[p] + part

    def c_arrives(s, i):
        from_chip(OF_C, s, c_half(flipped(chip, s) * 2 + core, i), i)

    def c_crosses(s):
        to_sib(OF_C, s, c_block(flipped(chip, s) * 2 + core))

    if two_hop:
        for s, i in ((1, 0), (2, 1)):
            c_arrives(s, i)
            part = c_half(flipped(chip, s) * 2 + core, i)
            to_chip(OF_C, 3, part, part, i, via=3 - s)
    start_half(chip, True)
    if two_hop:
        c_arrives(1, 1)
        c_crosses(1)
        c_arrives(2, 0)
        c_crosses(2)
    else:
        for s in steps[:-1]:
            c_arrives(s, 0)
            c_arrives(s, 1)
            c_crosses(s)
    for s in steps[:-1]:
        from_sib(OF_C, s, c_block(flipped(chip, s) * 2 + 1 - core))
        start_half(flipped(chip, s), False)
    c_last = flipped(chip, n_chip - 1)
    c_arrives(n_chip - 1, 0)
    c_arrives(n_chip - 1, 1)
    c_crosses(n_chip - 1)
    from_sib(OF_C, n_chip - 1, c_block(c_last * 2 + 1 - core))

    def end_half(p):
        h_own[p] = (acc[p] + half_part(p, c_last)).astype(BF16)

    def h_slot(c, a, i):
        return h_buf.at[c * aux + a * half_aux + i]

    def upper(s):
        top = 1 << (s.bit_length() - 1)
        return lax.rem(lax.div(chip, top), 2)

    def aux_from(s, i):
        if not two_hop:
            return half_aux * upper(s) + i
        ahead = 1 - bit1 if s > 1 else bit1
        if s == 3:
            return 2 * (parity if i == 0 else 1 - parity) + ahead
        return 2 * (1 - parity if s == 1 else parity) + (ahead if i == 0 else 1 - ahead)

    if two_hop:
        for s, i in ((1, 0), (2, 0), (1, 1), (2, 1)):
            p = 2 * (parity if s == 1 else 1 - parity) + (bit1 if i == 0 else 1 - bit1)
            end_half(p)
            to_chip(OF_H, s, h_own.at[p], h_slot(chip, core, i), i)
    else:
        pl.loop(0, aux)(end_half)
        for s in steps:
            for i in range(half_aux):
                to_chip(OF_H, s, h_own.at[half_aux * (1 - upper(s)) + i], h_slot(chip, core, i), i)
    own_slot = h_buf.at[pl.ds(chip * aux, aux)]
    send(h_own, own_slot, fwd_s.at[OF_H, 0, 0], fwd_r.at[OF_H, 0, 0], (z, sib))

    def pair(own_first, other, other_first, count):
        def add(p, total):
            return total + dot_nt(h_own[own_first + p], other[other_first + p])

        return lax.fori_loop(0, count, add, jnp.zeros((rows, rows), F32))

    k_block(b)[...] = pair(0, h_own, 0, aux)

    for s in range(1, n_grp):
        arrived(s_rows.at[flipped(z, s)], sz_s.at[s], sz_r.at[s])
    mid[:rows] = jnp.zeros((rows, mid.shape[1]), F32)

    @pl.loop(0, n_grp)
    def _(g):
        start = pl.multiple_of(g * width, width)
        mid[:rows] += dot_nn(s_rows[g], c_all[pl.ds(start, width), :])

    m_rows = (mid[:rows] * env_ref[...].astype(F32)).astype(BF16)

    @pl.loop(0, n_blk)
    def _(j):
        t_row(j)[...] = dot_nt(m_rows, c_block(j)[...]).astype(BF16)

    from_sib(OF_H, 0, own_slot)
    k_block(sib)[...] = pair(0, h_buf, chip * aux, aux)

    def sum_copy(c):
        return remote(k_send(c), k_recv.at[z], sum_s.at[c], sum_r.at[z], (c, b))

    def finish_chunk(c):
        for a in range(2):
            at = pl.multiple_of(c * width + a * rows, rows)
            slab[3, :, pl.ds(at, rows)] = k_block(2 * c + a)[...].astype(BF16)

        @pl.when(c != z)
        def _():
            sum_copy(c).start()

    finish_chunk(chip)

    def exchange_block(s, a):
        c = flipped(chip, s)
        other = 2 * c + a
        block = sum(dot_nt(h_own[aux_from(s, i)], h_slot(c, a, i)[...]) for i in range(half_aux))
        k_block(other)[...] = block
        zt_send[other] = block.T.astype(BF16)
        send(zt_send.at[other], zt_recv.at[b], zt_s.at[2 * s + a], zt_r.at[2 * s + core], (z, other))

    def add_block(s):
        c = flipped(chip, s)
        for a in range(2):
            other = 2 * c + a
            arrived(zt_recv.at[other], zt_s.at[2 * s + a], zt_r.at[2 * s + a])
            k_block(other)[...] += zt_recv[other].astype(F32)
        finish_chunk(c)

    def h_arrives(s, i):
        slot = h_slot(flipped(chip, s), core, i)
        from_chip(OF_H, s, slot, i)
        if two_hop and s < 3 and i == 0:
            to_chip(OF_H, 3, slot, h_slot(flipped(chip, s), core, s - 1), s - 1, via=3 - s)
        to_sib(OF_H, s, slot, i)

    def exchange_step(s):
        exchange_block(s, core)
        for i in range(half_aux):
            from_sib(OF_H, s, h_slot(flipped(chip, s), 1 - core, i), i)
        exchange_block(s, 1 - core)

    if two_hop:
        for s, i in ((1, 0), (2, 0), (1, 1), (2, 1)):
            h_arrives(s, i)
        exchange_step(1)
        exchange_step(2)
        add_block(1)
        add_block(2)
        h_arrives(3, 0)
        h_arrives(3, 1)
        exchange_step(3)
    else:
        for s in steps:
            for i in range(half_aux):
                h_arrives(s, i)
            exchange_step(s)
            if s > 1:
                add_block(s - 1)
    to_sib(OF_S, 0, s_cols.at[b])
    for s in steps:
        to_chip(OF_S, s, s_cols.at[b], s_cols.at[b])
    add_block(n_chip - 1)

    from_sib(OF_S, 0, s_cols.at[sib])
    for s in steps:
        c = flipped(chip, s)
        from_chip(OF_S, s, s_cols.at[2 * c + core])
        to_sib(OF_S, s, s_cols.at[2 * c + core])
    for s in steps:
        from_sib(OF_S, s, s_cols.at[2 * flipped(chip, s) + 1 - core])
    mid[...] = jnp.zeros(mid.shape, F32)

    @pl.loop(0, n_blk)
    def _(j):
        mid[...] += dot_tn(s_cols[j], c_block(j)[...])

    m_cols = (mid[...] * env_ref[...].astype(F32)).astype(BF16)

    @pl.loop(0, n_blk)
    def _(j):
        t_col(j)[...] = dot_nt(c_block(j)[...], m_cols).astype(BF16)

    k_tile = jnp.concatenate([k_block(2 * z)[...], k_block(2 * z + 1)[...]], axis=1)
    for s in range(1, n_grp):
        other = flipped(z, s)
        arrived(k_recv.at[other], sum_s.at[other], sum_r.at[other])
        k_tile = k_tile + k_recv[other].astype(F32)
    k_bf = k_tile.astype(BF16)
    out_ref[...] = k_tile
    k_cols[b] = k_bf
    k_rows[z] = k_bf
    line = n_grp == 4

    def row_copy(g, sems, to):
        return remote(k_rows.at[g], k_rows.at[g], sems.at[g], kz_r.at[g], (to, b))

    def pass_rows(g, ahead, wait):
        def act(copy):
            copy.wait_send() if wait else copy.start()

        if ahead > 0:
            pl.when(z < n_grp - 1)(lambda: act(row_copy(g, kz_up, z + 1)))
        else:
            pl.when(z > 0)(lambda: act(row_copy(g, kz_down, z - 1)))

    if line:
        pass_rows(z, 1, False)
        pass_rows(z, -1, False)
    else:
        for s in range(1, n_grp):
            send(k_rows.at[z], k_rows.at[z], kz_up.at[s], kz_r.at[s], (flipped(z, s), b))
    to_sib(OF_K, 0, k_cols.at[b])
    for s in steps:
        to_chip(OF_K, s, k_cols.at[b], k_cols.at[b])

    def take_first(j):
        out_ref[...] -= dot_nn(t_row(j)[...], k_cols[j])

    def take_second(g):
        out_ref[...] -= dot_nn(k_rows[g, :, :rows], t_col(2 * g)[...])
        out_ref[...] -= dot_nn(k_rows[g, :, rows:], t_col(2 * g + 1)[...])

    def line_rows(d, wait=False):
        for ahead in (1, -1):
            g = z - ahead * d

            @pl.when(z >= d if ahead > 0 else z < n_grp - d)
            def _():
                if not wait:
                    arrived(k_rows.at[g], kz_up.at[g], kz_r.at[g])
                pass_rows(g, ahead, wait)
                if not wait:
                    take_second(g)

    def cols_arrive(s):
        other = 2 * flipped(chip, s) + core
        from_chip(OF_K, s, k_cols.at[other])
        to_sib(OF_K, s, k_cols.at[other])
        take_first(other)

    take_first(b)
    take_second(z)
    from_sib(OF_K, 0, k_cols.at[sib])
    take_first(sib)
    if line:
        line_rows(1)
    for s in steps:
        cols_arrive(s)
        if line and s == 1:
            line_rows(2)
    for s in steps:
        other = 2 * flipped(chip, s) + 1 - core
        from_sib(OF_K, s, k_cols.at[other])
        take_first(other)
    if line:
        line_rows(3)
        pass_rows(z, 1, True)
        pass_rows(z, -1, True)
        line_rows(1, True)
        line_rows(2, True)
        line_rows(3, True)
    else:
        for s in range(1, n_grp):
            other = flipped(z, s)
            arrived(k_rows.at[other], kz_up.at[s], kz_r.at[s])
            take_second(other)

    for copy in sent:
        copy.wait_send()
    for s in range(n_chip):
        c = flipped(chip, s)

        @pl.when(c != z)
        def _():
            sum_copy(c).wait_send()


def on_device(n_grp, n_blk, slab, block_mask, orbitals, margin, env_flag):
    aux, rows, nao = slab.shape
    occ = orbitals.shape[1]
    width = margin.shape[1]
    n_chip = n_blk // 2
    assert width == 2 * rows and n_chip == n_grp and aux == 4
    env = env_flag[None, :]
    vmem = pl.BlockSpec(memory_space=pltpu.VMEM)
    dma = pltpu.SemaphoreType.DMA
    return pl.pallas_call(
        functools.partial(kernel, n_grp, n_blk),
        out_shape=jax.ShapeDtypeStruct((rows, width), F32),
        in_specs=[vmem] * 4 + [pl.BlockSpec(memory_space=pl.ANY)],
        out_specs=vmem,
        scratch_shapes=[
            pltpu.VMEM((aux, rows, nao), BF16),
            pltpu.VMEM((nao, occ), BF16),
            pltpu.VMEM((aux, rows, occ), F32),
            pltpu.VMEM((aux, rows, occ), BF16),
            pltpu.VMEM((n_chip * aux, rows, occ), BF16),
            pltpu.VMEM((n_blk, rows, rows), BF16),
            pltpu.VMEM((n_blk, rows, rows), BF16),
            pltpu.VMEM((n_grp, rows, width), BF16),
            pltpu.VMEM((n_blk, rows, width), BF16),
            pltpu.VMEM((n_grp, rows, width), BF16),
            pltpu.VMEM((n_blk, rows, width), BF16),
            pltpu.VMEM((n_grp, rows, width), BF16),
            pltpu.VMEM((width, occ), F32),
            dma(()),
            dma((4, n_chip, 2)), dma((4, n_chip, 2)), dma((4, n_chip, 2)), dma((4, n_chip, 2)),
            dma((2 * n_chip,)), dma((2 * n_chip,)),
            dma((n_grp,)), dma((n_grp,)), dma((n_grp,)), dma((n_grp,)), dma((n_grp,)), dma((n_grp,)),
            dma((n_grp,)),
        ],
        compiler_params=pltpu.CompilerParams(
            collective_id=0, has_side_effects=True, vmem_limit_bytes=63 * 2**20
        ),
    )(block_mask, env, orbitals, margin, slab)


def solution(mesh):
    placed = (P("grp", "blk", None), P("grp", "blk", None), P("blk", None), P("blk", "grp"), P())
    return jax.shard_map(
        functools.partial(on_device, mesh.shape["grp"], mesh.shape["blk"]),
        mesh=mesh, in_specs=placed, out_specs=P("blk", "grp"), check_vma=False,
    )
```

```python
import functools

import jax
import jax.numpy as jnp
from jax import lax
from jax.experimental import pallas as pl
from jax.experimental.pallas import tpu as pltpu
from jax.sharding import PartitionSpec as P

ATILE = 32
MESH = pl.DeviceIdType.MESH
BF16 = jnp.bfloat16
F32 = jnp.float32
OF_C, OF_H, OF_K, OF_S = range(4)


def dot_nn(left, right):
    return lax.dot_general(left, right, (((1,), (0,)), ((), ())), preferred_element_type=F32)


def dot_nt(left, right):
    return lax.dot_general(left, right, (((1,), (1,)), ((), ())), preferred_element_type=F32)


def dot_tn(left, right):
    return lax.dot_general(left, right, (((0,), (0,)), ((), ())), preferred_element_type=F32)


def flipped(index, step):
    bit = 1
    while bit <= step:
        if step & bit:
            index = index + bit - 2 * bit * lax.rem(lax.div(index, bit), 2)
        bit *= 2
    return index


def kernel(
    n_grp, n_blk,
    mask_ref, env_ref, orb_ref, margin_ref, slab_hbm, out_ref,
    slab, c_all, acc, h_own, h_buf, zt_send, zt_recv, k_recv,
    k_cols, k_rows, s_cols, s_rows, mid,
    load_sem, dir_s, dir_r, fwd_s, fwd_r, zt_s, zt_r, sum_s, sum_r, kz_up, kz_down, kz_r, sz_s, sz_r,
):
    z = lax.axis_index("grp")
    b = lax.axis_index("blk")
    n_chip = n_blk // 2
    chip, core = lax.div(b, 2), lax.rem(b, 2)
    sib = chip * 2 + 1 - core
    aux, rows, nao = slab.shape
    half_aux = aux // 2
    width = 2 * rows
    steps = range(1, n_chip)
    two_hop = n_chip == 4
    bit1 = lax.div(chip, 2)
    parity = lax.rem(lax.rem(chip, 2) + bit1, 2)
    sent = []

    load = pltpu.make_async_copy(slab_hbm, slab, load_sem)
    load.start()

    barrier = pltpu.get_barrier_semaphore()
    for s in range(1, n_blk):
        pl.semaphore_signal(barrier, inc=1, device_id=(z, lax.rem(b + s, n_blk)), device_id_type=MESH)
    for s in range(1, n_grp):
        pl.semaphore_signal(barrier, inc=1, device_id=(lax.rem(z + s, n_grp), b), device_id_type=MESH)
    pl.semaphore_wait(barrier, n_blk + n_grp - 2)

    def remote(src, dst, send_sem, recv_sem, to):
        return pltpu.make_async_remote_copy(
            src_ref=src, dst_ref=dst, send_sem=send_sem, recv_sem=recv_sem,
            device_id=to, device_id_type=MESH,
        )

    def send(src, dst, send_sem, recv_sem, to):
        copy = remote(src, dst, send_sem, recv_sem, to)
        copy.start()
        sent.append(copy)

    def arrived(dst, send_sem, recv_sem):
        remote(dst, dst, send_sem, recv_sem, (z, sib)).wait_recv()

    def to_chip(kind, s, src, dst, i=0, via=None):
        to = (z, flipped(chip, via or s) * 2 + core)
        send(src, dst, dir_s.at[kind, s, i], dir_r.at[kind, s, i], to)

    def from_chip(kind, s, dst, i=0):
        arrived(dst, dir_s.at[kind, s, i], dir_r.at[kind, s, i])

    def to_sib(kind, s, ref, i=0):
        send(ref, ref, fwd_s.at[kind, s, i], fwd_r.at[kind, s, i], (z, sib))

    def from_sib(kind, s, dst, i=0):
        arrived(dst, fwd_s.at[kind, s, i], fwd_r.at[kind, s, i])

    per_acc = acc.shape[2] // rows

    def k_block(j):
        start = pl.multiple_of(lax.rem(j, per_acc) * rows, rows)
        return acc.at[lax.div(j, per_acc), :, pl.ds(start, rows)]

    def t_row(j):
        return slab.at[2, :, pl.ds(pl.multiple_of(j * rows, rows), rows)]

    def t_col(j):
        start = pl.multiple_of(lax.rem(j, n_grp) * width, width)
        return slab.at[lax.div(j, n_grp), :, pl.ds(start, width)]

    def k_send(c):
        return slab.at[3, :, pl.ds(pl.multiple_of(c * width, width), width)]

    def c_block(index):
        return c_all.at[pl.ds(pl.multiple_of(index * rows, rows), rows)]

    c_block(b)[...] = orb_ref[...]
    to_sib(OF_C, 0, c_block(b))

    def c_half(index, i):
        start = pl.multiple_of(index * rows + i * (rows // 2), rows // 2)
        return c_all.at[pl.ds(start, rows // 2)]

    if two_hop:
        for s, i in ((1, 0), (2, 1), (1, 1), (2, 0)):
            to_chip(OF_C, s, c_half(b, i), c_half(b, i), i)
    else:
        for s in steps:
            for i in range(2):
                to_chip(OF_C, s, c_half(b, i), c_half(b, i), i)
    s_rows[z] = margin_ref[...]
    s_cols[b] = margin_ref[...]
    for s in range(1, n_grp):
        send(s_rows.at[z], s_rows.at[z], sz_s.at[s], sz_r.at[s], (flipped(z, s), b))

    spread = lax.broadcasted_iota(jnp.int32, (nao // ATILE, nao), 1)
    tile = lax.broadcasted_iota(jnp.int32, (nao // ATILE, nao), 0) * ATILE
    spread = jnp.where((spread >= tile) & (spread < tile + ATILE), 1.0, 0.0).astype(BF16)
    keep_all = dot_nn(mask_ref[0].astype(F32).astype(BF16), spread)
    load.wait()
    for t in range(rows // ATILE):
        keep = jnp.broadcast_to(keep_all[t : t + 1, :], (ATILE, nao)).astype(BF16)

        @pl.loop(0, aux)
        def _(p):
            slab[p, t * ATILE : (t + 1) * ATILE, :] = slab[p, t * ATILE : (t + 1) * ATILE, :] * keep

    def half_part(p, c):
        start = pl.multiple_of(c * width, width)
        return dot_nn(slab[p, :, pl.ds(start, width)], c_all[pl.ds(start, width), :])

    from_sib(OF_C, 0, c_block(sib))

    def start_half(c, first):
        @pl.loop(0, aux)
        def _(p):
            part = half_part(p, c)
            acc[p] = part if first else acc[p] + part

    def c_arrives(s, i):
        from_chip(OF_C, s, c_half(flipped(chip, s) * 2 + core, i), i)

    def c_crosses(s):
        to_sib(OF_C, s, c_block(flipped(chip, s) * 2 + core))

    if two_hop:
        for s, i in ((1, 0), (2, 1)):
            c_arrives(s, i)
            part = c_half(flipped(chip, s) * 2 + core, i)
            to_chip(OF_C, 3, part, part, i, via=3 - s)
    start_half(chip, True)
    if two_hop:
        c_arrives(1, 1)
        c_crosses(1)
        c_arrives(2, 0)
        c_crosses(2)
    else:
        for s in steps[:-1]:
            c_arrives(s, 0)
            c_arrives(s, 1)
            c_crosses(s)
    for s in steps[:-1]:
        from_sib(OF_C, s, c_block(flipped(chip, s) * 2 + 1 - core))
        start_half(flipped(chip, s), False)
    c_last = flipped(chip, n_chip - 1)
    c_arrives(n_chip - 1, 0)
    c_arrives(n_chip - 1, 1)
    c_crosses(n_chip - 1)
    from_sib(OF_C, n_chip - 1, c_block(c_last * 2 + 1 - core))

    def end_half(p):
        h_own[p] = (acc[p] + half_part(p, c_last)).astype(BF16)

    def h_slot(c, a, i):
        return h_buf.at[c * aux + a * half_aux + i]

    def upper(s):
        top = 1 << (s.bit_length() - 1)
        return lax.rem(lax.div(chip, top), 2)

    def aux_from(s, i):
        if not two_hop:
            return half_aux * upper(s) + i
        ahead = 1 - bit1 if s > 1 else bit1
        if s == 3:
            return 2 * (parity if i == 0 else 1 - parity) + ahead
        return 2 * (1 - parity if s == 1 else parity) + (ahead if i == 0 else 1 - ahead)

    if two_hop:
        for s, i in ((1, 0), (2, 0), (1, 1), (2, 1)):
            p = 2 * (parity if s == 1 else 1 - parity) + (bit1 if i == 0 else 1 - bit1)
            end_half(p)
            to_chip(OF_H, s, h_own.at[p], h_slot(chip, core, i), i)
    else:
        pl.loop(0, aux)(end_half)
        for s in steps:
            for i in range(half_aux):
                to_chip(OF_H, s, h_own.at[half_aux * (1 - upper(s)) + i], h_slot(chip, core, i), i)
    own_slot = h_buf.at[pl.ds(chip * aux, aux)]
    send(h_own, own_slot, fwd_s.at[OF_H, 0, 0], fwd_r.at[OF_H, 0, 0], (z, sib))

    def pair(own_first, other, other_first, count):
        def add(p, total):
            return total + dot_nt(h_own[own_first + p], other[other_first + p])

        return lax.fori_loop(0, count, add, jnp.zeros((rows, rows), F32))

    k_block(b)[...] = pair(0, h_own, 0, aux)

    for s in range(1, n_grp):
        arrived(s_rows.at[flipped(z, s)], sz_s.at[s], sz_r.at[s])
    mid[:rows] = jnp.zeros((rows, mid.shape[1]), F32)

    @pl.loop(0, n_grp)
    def _(g):
        start = pl.multiple_of(g * width, width)
        mid[:rows] += dot_nn(s_rows[g], c_all[pl.ds(start, width), :])

    m_rows = (mid[:rows] * env_ref[...].astype(F32)).astype(BF16)

    @pl.loop(0, n_blk)
    def _(j):
        t_row(j)[...] = dot_nt(m_rows, c_block(j)[...]).astype(BF16)

    from_sib(OF_H, 0, own_slot)
    k_block(sib)[...] = pair(0, h_buf, chip * aux, aux)

    def sum_copy(c):
        return remote(k_send(c), k_recv.at[z], sum_s.at[c], sum_r.at[z], (c, b))

    def finish_chunk(c):
        for a in range(2):
            at = pl.multiple_of(c * width + a * rows, rows)
            slab[3, :, pl.ds(at, rows)] = k_block(2 * c + a)[...].astype(BF16)

        @pl.when(c != z)
        def _():
            sum_copy(c).start()

    finish_chunk(chip)

    def exchange_block(s, a):
        c = flipped(chip, s)
        other = 2 * c + a
        block = sum(dot_nt(h_own[aux_from(s, i)], h_slot(c, a, i)[...]) for i in range(half_aux))
        k_block(other)[...] = block
        zt_send[other] = block.T.astype(BF16)
        send(zt_send.at[other], zt_recv.at[b], zt_s.at[2 * s + a], zt_r.at[2 * s + core], (z, other))

    def add_block(s):
        c = flipped(chip, s)
        for a in range(2):
            other = 2 * c + a
            arrived(zt_recv.at[other], zt_s.at[2 * s + a], zt_r.at[2 * s + a])
            k_block(other)[...] += zt_recv[other].astype(F32)
        finish_chunk(c)

    def h_arrives(s, i):
        slot = h_slot(flipped(chip, s), core, i)
        from_chip(OF_H, s, slot, i)
        to_sib(OF_H, s, slot, i)

    def exchange_step(s):
        exchange_block(s, core)
        for i in range(half_aux):
            from_sib(OF_H, s, h_slot(flipped(chip, s), 1 - core, i), i)
        exchange_block(s, 1 - core)

    if two_hop:
        for s, i in ((1, 0), (2, 0), (1, 1), (2, 1)):
            h_arrives(s, i)
        for s in (1, 2):
            c = flipped(chip, s)
            to_chip(OF_H, 3, h_slot(c, core, 0), h_slot(c, core, s - 1), s - 1, via=3 - s)
        exchange_step(1)
        exchange_step(2)
        add_block(1)
        add_block(2)
        h_arrives(3, 0)
        h_arrives(3, 1)
        exchange_step(3)
    else:
        for s in steps:
            for i in range(half_aux):
                h_arrives(s, i)
            exchange_step(s)
            if s > 1:
                add_block(s - 1)
    add_block(n_chip - 1)
    to_sib(OF_S, 0, s_cols.at[b])
    for s in steps:
        to_chip(OF_S, s, s_cols.at[b], s_cols.at[b])

    def add_margin(j):
        mid[...] += dot_tn(s_cols[j], c_block(j)[...])

    mid[...] = dot_tn(s_cols[b], c_block(b)[...])
    from_sib(OF_S, 0, s_cols.at[sib])
    add_margin(sib)
    for s in steps:
        other = 2 * flipped(chip, s)
        from_chip(OF_S, s, s_cols.at[other + core])
        to_sib(OF_S, s, s_cols.at[other + core])
        add_margin(other + core)
    for s in steps:
        other = 2 * flipped(chip, s) + 1 - core
        from_sib(OF_S, s, s_cols.at[other])
        add_margin(other)
    m_cols = (mid[...] * env_ref[...].astype(F32)).astype(BF16)

    k_tile = jnp.concatenate([k_block(2 * z)[...], k_block(2 * z + 1)[...]], axis=1)
    for s in range(1, n_grp):
        other = flipped(z, s)
        arrived(k_recv.at[other], sum_s.at[other], sum_r.at[other])
        k_tile = k_tile + k_recv[other].astype(F32)
    k_bf = k_tile.astype(BF16)
    out_ref[...] = k_tile
    k_cols[b] = k_bf
    k_rows[z] = k_bf
    line = n_grp == 4

    def row_copy(g, sems, to):
        return remote(k_rows.at[g], k_rows.at[g], sems.at[g], kz_r.at[g], (to, b))

    def pass_rows(g, ahead, wait):
        def act(copy):
            copy.wait_send() if wait else copy.start()

        if ahead > 0:
            pl.when(z < n_grp - 1)(lambda: act(row_copy(g, kz_up, z + 1)))
        else:
            pl.when(z > 0)(lambda: act(row_copy(g, kz_down, z - 1)))

    if line:
        pass_rows(z, 1, False)
        pass_rows(z, -1, False)
    else:
        for s in range(1, n_grp):
            send(k_rows.at[z], k_rows.at[z], kz_up.at[s], kz_r.at[s], (flipped(z, s), b))
    to_sib(OF_K, 0, k_cols.at[b])
    for s in steps:
        to_chip(OF_K, s, k_cols.at[b], k_cols.at[b])

    @pl.loop(0, n_blk)
    def _(j):
        t_col(j)[...] = dot_nt(c_block(j)[...], m_cols).astype(BF16)

    def take_first(j):
        out_ref[...] -= dot_nn(t_row(j)[...], k_cols[j])

    def take_second(g):
        out_ref[...] -= dot_nn(k_rows[g, :, :rows], t_col(2 * g)[...])
        out_ref[...] -= dot_nn(k_rows[g, :, rows:], t_col(2 * g + 1)[...])

    def line_rows(d, wait=False):
        for ahead in (1, -1):
            g = z - ahead * d

            @pl.when(z >= d if ahead > 0 else z < n_grp - d)
            def _():
                if not wait:
                    arrived(k_rows.at[g], kz_up.at[g], kz_r.at[g])
                pass_rows(g, ahead, wait)
                if not wait:
                    take_second(g)

    def cols_arrive(s):
        other = 2 * flipped(chip, s) + core
        from_chip(OF_K, s, k_cols.at[other])
        to_sib(OF_K, s, k_cols.at[other])
        take_first(other)

    take_first(b)
    take_second(z)
    from_sib(OF_K, 0, k_cols.at[sib])
    take_first(sib)
    if line:
        line_rows(1)
    for s in steps:
        cols_arrive(s)
        if line and s == 1:
            line_rows(2)
    for s in steps:
        other = 2 * flipped(chip, s) + 1 - core
        from_sib(OF_K, s, k_cols.at[other])
        take_first(other)
    if line:
        line_rows(3)
        pass_rows(z, 1, True)
        pass_rows(z, -1, True)
        line_rows(1, True)
        line_rows(2, True)
        line_rows(3, True)
    else:
        for s in range(1, n_grp):
            other = flipped(z, s)
            arrived(k_rows.at[other], kz_up.at[s], kz_r.at[s])
            take_second(other)

    for copy in sent:
        copy.wait_send()
    for s in range(n_chip):
        c = flipped(chip, s)

        @pl.when(c != z)
        def _():
            sum_copy(c).wait_send()


def on_device(n_grp, n_blk, slab, block_mask, orbitals, margin, env_flag):
    aux, rows, nao = slab.shape
    occ = orbitals.shape[1]
    width = margin.shape[1]
    n_chip = n_blk // 2
    assert width == 2 * rows and n_chip == n_grp and aux == 4
    env = env_flag[None, :]
    vmem = pl.BlockSpec(memory_space=pltpu.VMEM)
    dma = pltpu.SemaphoreType.DMA
    return pl.pallas_call(
        functools.partial(kernel, n_grp, n_blk),
        out_shape=jax.ShapeDtypeStruct((rows, width), F32),
        in_specs=[vmem] * 4 + [pl.BlockSpec(memory_space=pl.ANY)],
        out_specs=vmem,
        scratch_shapes=[
            pltpu.VMEM((aux, rows, nao), BF16),
            pltpu.VMEM((nao, occ), BF16),
            pltpu.VMEM((aux, rows, occ), F32),
            pltpu.VMEM((aux, rows, occ), BF16),
            pltpu.VMEM((n_chip * aux, rows, occ), BF16),
            pltpu.VMEM((n_blk, rows, rows), BF16),
            pltpu.VMEM((n_blk, rows, rows), BF16),
            pltpu.VMEM((n_grp, rows, width), BF16),
            pltpu.VMEM((n_blk, rows, width), BF16),
            pltpu.VMEM((n_grp, rows, width), BF16),
            pltpu.VMEM((n_blk, rows, width), BF16),
            pltpu.VMEM((n_grp, rows, width), BF16),
            pltpu.VMEM((width, occ), F32),
            dma(()),
            dma((4, n_chip, 2)), dma((4, n_chip, 2)), dma((4, n_chip, 2)), dma((4, n_chip, 2)),
            dma((2 * n_chip,)), dma((2 * n_chip,)),
            dma((n_grp,)), dma((n_grp,)), dma((n_grp,)), dma((n_grp,)), dma((n_grp,)), dma((n_grp,)),
            dma((n_grp,)),
        ],
        compiler_params=pltpu.CompilerParams(
            collective_id=0, has_side_effects=True, vmem_limit_bytes=63 * 2**20
        ),
    )(block_mask, env, orbitals, margin, slab)


def solution(mesh):
    placed = (P("grp", "blk", None), P("grp", "blk", None), P("blk", None), P("blk", "grp"), P())
    return jax.shard_map(
        functools.partial(on_device, mesh.shape["grp"], mesh.shape["blk"]),
        mesh=mesh, in_specs=placed, out_specs=P("blk", "grp"), check_vma=False,
    )
```

```python
import functools

import jax
import jax.numpy as jnp
from jax import lax
from jax.experimental import pallas as pl
from jax.experimental.pallas import tpu as pltpu
from jax.sharding import PartitionSpec as P

ATILE = 32
MESH = pl.DeviceIdType.MESH
BF16 = jnp.bfloat16
F32 = jnp.float32
OF_C, OF_H, OF_K, OF_S = range(4)


def dot_nn(left, right):
    return lax.dot_general(left, right, (((1,), (0,)), ((), ())), preferred_element_type=F32)


def dot_nt(left, right):
    return lax.dot_general(left, right, (((1,), (1,)), ((), ())), preferred_element_type=F32)


def dot_tn(left, right):
    return lax.dot_general(left, right, (((0,), (0,)), ((), ())), preferred_element_type=F32)


def flipped(index, step):
    bit = 1
    while bit <= step:
        if step & bit:
            index = index + bit - 2 * bit * lax.rem(lax.div(index, bit), 2)
        bit *= 2
    return index


def kernel(
    n_grp, n_blk,
    mask_ref, env_ref, orb_ref, margin_ref, slab_hbm, tile_ref, fix_ref,
    slab, c_all, acc, h_own, h_buf, zt_send, zt_recv, k_recv,
    k_cols, k_rows, s_cols, s_rows, mid,
    load_sem, dir_s, dir_r, fwd_s, fwd_r, zt_s, zt_r, sum_s, sum_r, kz_up, kz_down, kz_r, sz_s, sz_r,
):
    z = lax.axis_index("grp")
    b = lax.axis_index("blk")
    n_chip = n_blk // 2
    chip, core = lax.div(b, 2), lax.rem(b, 2)
    sib = chip * 2 + 1 - core
    aux, rows, nao = slab.shape
    half_aux = aux // 2
    width = 2 * rows
    steps = range(1, n_chip)
    two_hop = n_chip == 4
    bit1 = lax.div(chip, 2)
    parity = lax.rem(lax.rem(chip, 2) + bit1, 2)
    sent = []

    load = pltpu.make_async_copy(slab_hbm, slab, load_sem)
    load.start()

    barrier = pltpu.get_barrier_semaphore()
    for s in range(1, n_blk):
        pl.semaphore_signal(barrier, inc=1, device_id=(z, lax.rem(b + s, n_blk)), device_id_type=MESH)
    for s in range(1, n_grp):
        pl.semaphore_signal(barrier, inc=1, device_id=(lax.rem(z + s, n_grp), b), device_id_type=MESH)
    pl.semaphore_wait(barrier, n_blk + n_grp - 2)

    def remote(src, dst, send_sem, recv_sem, to):
        return pltpu.make_async_remote_copy(
            src_ref=src, dst_ref=dst, send_sem=send_sem, recv_sem=recv_sem,
            device_id=to, device_id_type=MESH,
        )

    def send(src, dst, send_sem, recv_sem, to):
        copy = remote(src, dst, send_sem, recv_sem, to)
        copy.start()
        sent.append(copy)

    def arrived(dst, send_sem, recv_sem):
        remote(dst, dst, send_sem, recv_sem, (z, sib)).wait_recv()

    def to_chip(kind, s, src, dst, i=0, via=None):
        to = (z, flipped(chip, via or s) * 2 + core)
        send(src, dst, dir_s.at[kind, s, i], dir_r.at[kind, s, i], to)

    def from_chip(kind, s, dst, i=0):
        arrived(dst, dir_s.at[kind, s, i], dir_r.at[kind, s, i])

    def to_sib(kind, s, ref, i=0):
        send(ref, ref, fwd_s.at[kind, s, i], fwd_r.at[kind, s, i], (z, sib))

    def from_sib(kind, s, dst, i=0):
        arrived(dst, fwd_s.at[kind, s, i], fwd_r.at[kind, s, i])

    per_acc = acc.shape[2] // rows

    def k_block(j):
        start = pl.multiple_of(lax.rem(j, per_acc) * rows, rows)
        return acc.at[lax.div(j, per_acc), :, pl.ds(start, rows)]

    def t_row(j):
        return slab.at[2, :, pl.ds(pl.multiple_of(j * rows, rows), rows)]

    def t_col(j):
        start = pl.multiple_of(lax.rem(j, n_grp) * width, width)
        return slab.at[lax.div(j, n_grp), :, pl.ds(start, width)]

    def k_send(c):
        return slab.at[3, :, pl.ds(pl.multiple_of(c * width, width), width)]

    def c_block(index):
        return c_all.at[pl.ds(pl.multiple_of(index * rows, rows), rows)]

    c_block(b)[...] = orb_ref[...]
    to_sib(OF_C, 0, c_block(b))

    def c_half(index, i):
        start = pl.multiple_of(index * rows + i * (rows // 2), rows // 2)
        return c_all.at[pl.ds(start, rows // 2)]

    if two_hop:
        for s, i in ((1, 0), (2, 1), (1, 1), (2, 0)):
            to_chip(OF_C, s, c_half(b, i), c_half(b, i), i)
    else:
        for s in steps:
            for i in range(2):
                to_chip(OF_C, s, c_half(b, i), c_half(b, i), i)
    s_rows[z] = margin_ref[...]
    s_cols[b] = margin_ref[...]
    for s in range(1, n_grp):
        send(s_rows.at[z], s_rows.at[z], sz_s.at[s], sz_r.at[s], (flipped(z, s), b))

    spread = lax.broadcasted_iota(jnp.int32, (nao // ATILE, nao), 1)
    tile = lax.broadcasted_iota(jnp.int32, (nao // ATILE, nao), 0) * ATILE
    spread = jnp.where((spread >= tile) & (spread < tile + ATILE), 1.0, 0.0).astype(BF16)
    keep_all = dot_nn(mask_ref[0].astype(F32).astype(BF16), spread)
    load.wait()
    for t in range(rows // ATILE):
        keep = jnp.broadcast_to(keep_all[t : t + 1, :], (ATILE, nao)).astype(BF16)

        @pl.loop(0, aux)
        def _(p):
            slab[p, t * ATILE : (t + 1) * ATILE, :] = slab[p, t * ATILE : (t + 1) * ATILE, :] * keep

    def half_part(p, c):
        start = pl.multiple_of(c * width, width)
        return dot_nn(slab[p, :, pl.ds(start, width)], c_all[pl.ds(start, width), :])

    from_sib(OF_C, 0, c_block(sib))

    def start_half(c, first):
        @pl.loop(0, aux)
        def _(p):
            part = half_part(p, c)
            acc[p] = part if first else acc[p] + part

    def c_arrives(s, i):
        from_chip(OF_C, s, c_half(flipped(chip, s) * 2 + core, i), i)

    def c_crosses(s):
        to_sib(OF_C, s, c_block(flipped(chip, s) * 2 + core))

    if two_hop:
        for s, i in ((1, 0), (2, 1)):
            c_arrives(s, i)
            part = c_half(flipped(chip, s) * 2 + core, i)
            to_chip(OF_C, 3, part, part, i, via=3 - s)
    start_half(chip, True)
    if two_hop:
        c_arrives(1, 1)
        c_crosses(1)
        c_arrives(2, 0)
        c_crosses(2)
    else:
        for s in steps[:-1]:
            c_arrives(s, 0)
            c_arrives(s, 1)
            c_crosses(s)
    for s in steps[:-1]:
        from_sib(OF_C, s, c_block(flipped(chip, s) * 2 + 1 - core))
        start_half(flipped(chip, s), False)
    c_last = flipped(chip, n_chip - 1)
    near, far = c_last * 2 + core, c_last * 2 + 1 - core
    for i in range(2):
        c_arrives(n_chip - 1, i)
        to_sib(OF_C, n_chip - 1, c_half(near, i), i)

    def block_part(p, j):
        start = pl.multiple_of(j * rows, rows)
        return dot_nn(slab[p, :, pl.ds(start, rows)], c_block(j)[...])

    @pl.loop(0, aux)
    def _(p):
        acc[p] = acc[p] + block_part(p, near)

    for i in range(2):
        from_sib(OF_C, n_chip - 1, c_half(far, i), i)

    def end_half(p):
        h_own[p] = (acc[p] + block_part(p, far)).astype(BF16)

    def h_slot(c, a, i):
        return h_buf.at[c * aux + a * half_aux + i]

    def upper(s):
        top = 1 << (s.bit_length() - 1)
        return lax.rem(lax.div(chip, top), 2)

    def aux_from(s, i):
        if not two_hop:
            return half_aux * upper(s) + i
        ahead = 1 - bit1 if s > 1 else bit1
        if s == 3:
            return 2 * (parity if i == 0 else 1 - parity) + ahead
        return 2 * (1 - parity if s == 1 else parity) + (ahead if i == 0 else 1 - ahead)

    def aux_to(s, i):
        return 2 * (parity if s == 1 else 1 - parity) + (bit1 if i == 0 else 1 - bit1)

    if two_hop:
        for s, i in ((1, 0), (2, 0)):
            end_half(aux_to(s, i))
            to_chip(OF_H, s, h_own.at[aux_to(s, i)], h_slot(chip, core, i), i)
        for s, i in ((1, 1), (2, 1)):
            end_half(aux_to(s, i))
    else:
        pl.loop(0, aux)(end_half)
        for s in steps:
            for i in range(half_aux):
                to_chip(OF_H, s, h_own.at[half_aux * (1 - upper(s)) + i], h_slot(chip, core, i), i)
    own_slot = h_buf.at[pl.ds(chip * aux, aux)]
    send(h_own, own_slot, fwd_s.at[OF_H, 0, 0], fwd_r.at[OF_H, 0, 0], (z, sib))

    def pair(own_first, other, other_first, count):
        def add(p, total):
            return total + dot_nt(h_own[own_first + p], other[other_first + p])

        return lax.fori_loop(0, count, add, jnp.zeros((rows, rows), F32))

    k_block(b)[...] = pair(0, h_own, 0, aux)

    for s in range(1, n_grp):
        arrived(s_rows.at[flipped(z, s)], sz_s.at[s], sz_r.at[s])
    mid[:rows] = jnp.zeros((rows, mid.shape[1]), F32)

    @pl.loop(0, n_grp)
    def _(g):
        start = pl.multiple_of(g * width, width)
        mid[:rows] += dot_nn(s_rows[g], c_all[pl.ds(start, width), :])

    m_rows = (mid[:rows] * env_ref[...].astype(F32)).astype(BF16)

    @pl.loop(0, n_blk)
    def _(j):
        t_row(j)[...] = dot_nt(m_rows, c_block(j)[...]).astype(BF16)

    from_sib(OF_H, 0, own_slot)
    k_block(sib)[...] = pair(0, h_buf, chip * aux, aux)

    def sum_copy(c):
        return remote(k_send(c), k_recv.at[z], sum_s.at[c], sum_r.at[z], (c, b))

    def finish_chunk(c):
        for a in range(2):
            at = pl.multiple_of(c * width + a * rows, rows)
            slab[3, :, pl.ds(at, rows)] = k_block(2 * c + a)[...].astype(BF16)

        @pl.when(c != z)
        def _():
            sum_copy(c).start()

    finish_chunk(chip)

    def exchange_block(s, a):
        c = flipped(chip, s)
        other = 2 * c + a
        block = sum(dot_nt(h_own[aux_from(s, i)], h_slot(c, a, i)[...]) for i in range(half_aux))
        k_block(other)[...] = block
        zt_send[other] = block.T.astype(BF16)
        send(zt_send.at[other], zt_recv.at[b], zt_s.at[2 * s + a], zt_r.at[2 * s + core], (z, other))

    def add_block(s):
        c = flipped(chip, s)
        for a in range(2):
            other = 2 * c + a
            arrived(zt_recv.at[other], zt_s.at[2 * s + a], zt_r.at[2 * s + a])
            k_block(other)[...] += zt_recv[other].astype(F32)
        finish_chunk(c)

    def h_arrives(s, i):
        slot = h_slot(flipped(chip, s), core, i)
        from_chip(OF_H, s, slot, i)
        to_sib(OF_H, s, slot, i)

    def exchange_step(s):
        exchange_block(s, core)
        for i in range(half_aux):
            from_sib(OF_H, s, h_slot(flipped(chip, s), 1 - core, i), i)
        exchange_block(s, 1 - core)

    if two_hop:
        for s in (1, 2):
            c = flipped(chip, s)
            slot = h_slot(c, core, 0)
            from_chip(OF_H, s, slot)
            to_chip(OF_H, 3, slot, h_slot(c, core, s - 1), s - 1, via=3 - s)
        for s in (1, 2):
            to_chip(OF_H, s, h_own.at[aux_to(s, 1)], h_slot(chip, core, 1), 1)
            to_sib(OF_H, s, h_slot(flipped(chip, s), core, 0))
        h_arrives(3, 0)
        h_arrives(3, 1)
        exchange_step(3)
        add_block(3)
        h_arrives(1, 1)
        h_arrives(2, 1)
        exchange_step(1)
        exchange_step(2)
        add_block(1)
        add_block(2)
    else:
        for s in steps:
            for i in range(half_aux):
                h_arrives(s, i)
            exchange_step(s)
            if s > 1:
                add_block(s - 1)
        add_block(n_chip - 1)
    to_sib(OF_S, 0, s_cols.at[b])
    for s in steps:
        to_chip(OF_S, s, s_cols.at[b], s_cols.at[b])

    def add_margin(j):
        mid[...] += dot_tn(s_cols[j], c_block(j)[...])

    mid[...] = dot_tn(s_cols[b], c_block(b)[...])
    from_sib(OF_S, 0, s_cols.at[sib])
    add_margin(sib)
    for s in steps:
        other = 2 * flipped(chip, s)
        from_chip(OF_S, s, s_cols.at[other + core])
        to_sib(OF_S, s, s_cols.at[other + core])
        add_margin(other + core)
    for s in steps:
        other = 2 * flipped(chip, s) + 1 - core
        from_sib(OF_S, s, s_cols.at[other])
        add_margin(other)
    m_cols = (mid[...] * env_ref[...].astype(F32)).astype(BF16)

    k_tile = jnp.concatenate([k_block(2 * z)[...], k_block(2 * z + 1)[...]], axis=1)
    for s in range(1, n_grp):
        other = flipped(z, s)
        arrived(k_recv.at[other], sum_s.at[other], sum_r.at[other])
        k_tile = k_tile + k_recv[other].astype(F32)
    k_bf = k_tile.astype(BF16)
    tile_ref[...] = k_tile
    k_cols[b] = k_bf
    k_rows[z] = k_bf
    line = n_grp == 4

    def row_copy(g, sems, to):
        return remote(k_rows.at[g], k_rows.at[g], sems.at[g], kz_r.at[g], (to, b))

    def pass_rows(g, ahead, wait):
        def act(copy):
            copy.wait_send() if wait else copy.start()

        if ahead > 0:
            pl.when(z < n_grp - 1)(lambda: act(row_copy(g, kz_up, z + 1)))
        else:
            pl.when(z > 0)(lambda: act(row_copy(g, kz_down, z - 1)))

    if line:
        pass_rows(z, 1, False)
        pass_rows(z, -1, False)
    else:
        for s in range(1, n_grp):
            send(k_rows.at[z], k_rows.at[z], kz_up.at[s], kz_r.at[s], (flipped(z, s), b))
    to_sib(OF_K, 0, k_cols.at[b])
    for s in steps:
        to_chip(OF_K, s, k_cols.at[b], k_cols.at[b])

    @pl.loop(0, n_blk)
    def _(j):
        t_col(j)[...] = dot_nt(c_block(j)[...], m_cols).astype(BF16)

    def take_first(j):
        fix_ref[...] += dot_nn(t_row(j)[...], k_cols[j])

    def take_second(g):
        fix_ref[...] += dot_nn(k_rows[g, :, :rows], t_col(2 * g)[...])
        fix_ref[...] += dot_nn(k_rows[g, :, rows:], t_col(2 * g + 1)[...])

    def line_rows(d, wait=False):
        for ahead in (1, -1):
            g = z - ahead * d

            @pl.when(z >= d if ahead > 0 else z < n_grp - d)
            def _():
                if not wait:
                    arrived(k_rows.at[g], kz_up.at[g], kz_r.at[g])
                pass_rows(g, ahead, wait)
                if not wait:
                    take_second(g)

    def cols_arrive(s):
        other = 2 * flipped(chip, s) + core
        from_chip(OF_K, s, k_cols.at[other])
        to_sib(OF_K, s, k_cols.at[other])
        take_first(other)

    fix_ref[...] = dot_nn(t_row(b)[...], k_bf)
    take_second(z)
    from_sib(OF_K, 0, k_cols.at[sib])
    take_first(sib)
    if line:
        line_rows(1)
    for s in steps:
        cols_arrive(s)
        if line and s == 1:
            line_rows(2)
    for s in steps:
        other = 2 * flipped(chip, s) + 1 - core
        from_sib(OF_K, s, k_cols.at[other])
        take_first(other)
    if line:
        line_rows(3)
        pass_rows(z, 1, True)
        pass_rows(z, -1, True)
        line_rows(1, True)
        line_rows(2, True)
        line_rows(3, True)
    else:
        for s in range(1, n_grp):
            other = flipped(z, s)
            arrived(k_rows.at[other], kz_up.at[s], kz_r.at[s])
            take_second(other)

    for copy in sent:
        copy.wait_send()
    for s in range(n_chip):
        c = flipped(chip, s)

        @pl.when(c != z)
        def _():
            sum_copy(c).wait_send()


def on_device(n_grp, n_blk, slab, block_mask, orbitals, margin, env_flag):
    aux, rows, nao = slab.shape
    occ = orbitals.shape[1]
    width = margin.shape[1]
    n_chip = n_blk // 2
    assert width == 2 * rows and n_chip == n_grp and aux == 4
    env = env_flag[None, :]
    vmem = pl.BlockSpec(memory_space=pltpu.VMEM)
    dma = pltpu.SemaphoreType.DMA
    tile, fix = pl.pallas_call(
        functools.partial(kernel, n_grp, n_blk),
        out_shape=[jax.ShapeDtypeStruct((rows, width), F32)] * 2,
        in_specs=[vmem] * 4 + [pl.BlockSpec(memory_space=pl.ANY)],
        out_specs=[vmem, vmem],
        scratch_shapes=[
            pltpu.VMEM((aux, rows, nao), BF16),
            pltpu.VMEM((nao, occ), BF16),
            pltpu.VMEM((aux, rows, occ), F32),
            pltpu.VMEM((aux, rows, occ), BF16),
            pltpu.VMEM((n_chip * aux, rows, occ), BF16),
            pltpu.VMEM((n_blk, rows, rows), BF16),
            pltpu.VMEM((n_blk, rows, rows), BF16),
            pltpu.VMEM((n_grp, rows, width), BF16),
            pltpu.VMEM((n_blk, rows, width), BF16),
            pltpu.VMEM((n_grp, rows, width), BF16),
            pltpu.VMEM((n_blk, rows, width), BF16),
            pltpu.VMEM((n_grp, rows, width), BF16),
            pltpu.VMEM((width, occ), F32),
            dma(()),
            dma((4, n_chip, 2)), dma((4, n_chip, 2)), dma((4, n_chip, 2)), dma((4, n_chip, 2)),
            dma((2 * n_chip,)), dma((2 * n_chip,)),
            dma((n_grp,)), dma((n_grp,)), dma((n_grp,)), dma((n_grp,)), dma((n_grp,)), dma((n_grp,)),
            dma((n_grp,)),
        ],
        compiler_params=pltpu.CompilerParams(
            collective_id=0, has_side_effects=True, vmem_limit_bytes=63 * 2**20
        ),
    )(block_mask, env, orbitals, margin, slab)
    return tile - fix


def solution(mesh):
    placed = (P("grp", "blk", None), P("grp", "blk", None), P("blk", None), P("blk", "grp"), P())
    return jax.shard_map(
        functools.partial(on_device, mesh.shape["grp"], mesh.shape["blk"]),
        mesh=mesh, in_specs=placed, out_specs=P("blk", "grp"), check_vma=False,
    )
```

```python
import functools

import jax
import jax.numpy as jnp
from jax import lax
from jax.experimental import pallas as pl
from jax.experimental.pallas import tpu as pltpu
from jax.sharding import PartitionSpec as P

ATILE = 32
MESH = pl.DeviceIdType.MESH
BF16 = jnp.bfloat16
F32 = jnp.float32
OF_C, OF_H, OF_K, OF_S = range(4)


def dot_nn(left, right):
    return lax.dot_general(left, right, (((1,), (0,)), ((), ())), preferred_element_type=F32)


def dot_nt(left, right):
    return lax.dot_general(left, right, (((1,), (1,)), ((), ())), preferred_element_type=F32)


def dot_tn(left, right):
    return lax.dot_general(left, right, (((0,), (0,)), ((), ())), preferred_element_type=F32)


def flipped(index, step):
    bit = 1
    while bit <= step:
        if step & bit:
            index = index + bit - 2 * bit * lax.rem(lax.div(index, bit), 2)
        bit *= 2
    return index


def kernel(
    n_grp, n_blk,
    mask_ref, env_ref, orb_ref, margin_ref, slab_hbm, out_ref,
    slab, c_all, acc, h_own, h_buf, zt_send, zt_recv, k_recv,
    k_cols, k_rows, s_cols, s_rows, mid, k_far,
    load_sem, dir_s, dir_r, fwd_s, fwd_r, zt_s, zt_r, sum_s, sum_r, kz_up, kz_down, kz_r, sz_s, sz_r, far_s, far_r,
):
    z = lax.axis_index("grp")
    b = lax.axis_index("blk")
    n_chip = n_blk // 2
    chip, core = lax.div(b, 2), lax.rem(b, 2)
    sib = chip * 2 + 1 - core
    aux, rows, nao = slab.shape
    half_aux = aux // 2
    width = 2 * rows
    steps = range(1, n_chip)
    two_hop = n_chip == 4
    bit1 = lax.div(chip, 2)
    parity = lax.rem(lax.rem(chip, 2) + bit1, 2)
    sent = []

    load = pltpu.make_async_copy(slab_hbm, slab, load_sem)
    load.start()

    barrier = pltpu.get_barrier_semaphore()
    for s in range(1, n_blk):
        pl.semaphore_signal(barrier, inc=1, device_id=(z, lax.rem(b + s, n_blk)), device_id_type=MESH)
    for s in range(1, n_grp):
        pl.semaphore_signal(barrier, inc=1, device_id=(lax.rem(z + s, n_grp), b), device_id_type=MESH)
    pl.semaphore_wait(barrier, n_blk + n_grp - 2)

    def remote(src, dst, send_sem, recv_sem, to):
        return pltpu.make_async_remote_copy(
            src_ref=src, dst_ref=dst, send_sem=send_sem, recv_sem=recv_sem,
            device_id=to, device_id_type=MESH,
        )

    def send(src, dst, send_sem, recv_sem, to):
        copy = remote(src, dst, send_sem, recv_sem, to)
        copy.start()
        sent.append(copy)

    def arrived(dst, send_sem, recv_sem):
        remote(dst, dst, send_sem, recv_sem, (z, sib)).wait_recv()

    def to_chip(kind, s, src, dst, i=0, via=None):
        to = (z, flipped(chip, via or s) * 2 + core)
        send(src, dst, dir_s.at[kind, s, i], dir_r.at[kind, s, i], to)

    def from_chip(kind, s, dst, i=0):
        arrived(dst, dir_s.at[kind, s, i], dir_r.at[kind, s, i])

    def to_sib(kind, s, ref, i=0):
        send(ref, ref, fwd_s.at[kind, s, i], fwd_r.at[kind, s, i], (z, sib))

    def from_sib(kind, s, dst, i=0):
        arrived(dst, fwd_s.at[kind, s, i], fwd_r.at[kind, s, i])

    per_acc = acc.shape[2] // rows

    def k_block(j):
        start = pl.multiple_of(lax.rem(j, per_acc) * rows, rows)
        return acc.at[lax.div(j, per_acc), :, pl.ds(start, rows)]

    def t_row(j):
        return slab.at[2, :, pl.ds(pl.multiple_of(j * rows, rows), rows)]

    def t_col(j):
        start = pl.multiple_of(lax.rem(j, n_grp) * width, width)
        return slab.at[lax.div(j, n_grp), :, pl.ds(start, width)]

    def k_send(c):
        return slab.at[3, :, pl.ds(pl.multiple_of(c * width, width), width)]

    def c_block(index):
        return c_all.at[pl.ds(pl.multiple_of(index * rows, rows), rows)]

    c_block(b)[...] = orb_ref[...]
    to_sib(OF_C, 0, c_block(b))

    def c_half(index, i):
        start = pl.multiple_of(index * rows + i * (rows // 2), rows // 2)
        return c_all.at[pl.ds(start, rows // 2)]

    if two_hop:
        for s, i in ((1, 0), (2, 1), (1, 1), (2, 0)):
            to_chip(OF_C, s, c_half(b, i), c_half(b, i), i)
    else:
        for s in steps:
            for i in range(2):
                to_chip(OF_C, s, c_half(b, i), c_half(b, i), i)
    s_rows[z] = margin_ref[...]
    s_cols[b] = margin_ref[...]
    for s in range(1, n_grp):
        send(s_rows.at[z], s_rows.at[z], sz_s.at[s], sz_r.at[s], (flipped(z, s), b))

    spread = lax.broadcasted_iota(jnp.int32, (nao // ATILE, nao), 1)
    tile = lax.broadcasted_iota(jnp.int32, (nao // ATILE, nao), 0) * ATILE
    spread = jnp.where((spread >= tile) & (spread < tile + ATILE), 1.0, 0.0).astype(BF16)
    keep_all = dot_nn(mask_ref[0].astype(F32).astype(BF16), spread)
    load.wait()
    for t in range(rows // ATILE):
        keep = jnp.broadcast_to(keep_all[t : t + 1, :], (ATILE, nao)).astype(BF16)

        @pl.loop(0, aux)
        def _(p):
            slab[p, t * ATILE : (t + 1) * ATILE, :] = slab[p, t * ATILE : (t + 1) * ATILE, :] * keep

    def half_part(p, c):
        start = pl.multiple_of(c * width, width)
        return dot_nn(slab[p, :, pl.ds(start, width)], c_all[pl.ds(start, width), :])

    from_sib(OF_C, 0, c_block(sib))

    def start_half(c, first):
        @pl.loop(0, aux)
        def _(p):
            part = half_part(p, c)
            acc[p] = part if first else acc[p] + part

    def c_arrives(s, i):
        from_chip(OF_C, s, c_half(flipped(chip, s) * 2 + core, i), i)

    def c_crosses(s):
        to_sib(OF_C, s, c_block(flipped(chip, s) * 2 + core))

    if two_hop:
        for s, i in ((1, 0), (2, 1)):
            c_arrives(s, i)
            part = c_half(flipped(chip, s) * 2 + core, i)
            to_chip(OF_C, 3, part, part, i, via=3 - s)
    start_half(chip, True)
    if two_hop:
        c_arrives(1, 1)
        c_crosses(1)
        c_arrives(2, 0)
        c_crosses(2)
    else:
        for s in steps[:-1]:
            c_arrives(s, 0)
            c_arrives(s, 1)
            c_crosses(s)
    for s in steps[:-1]:
        from_sib(OF_C, s, c_block(flipped(chip, s) * 2 + 1 - core))
        start_half(flipped(chip, s), False)
    c_last = flipped(chip, n_chip - 1)
    near, far = c_last * 2 + core, c_last * 2 + 1 - core
    for i in range(2):
        c_arrives(n_chip - 1, i)
        to_sib(OF_C, n_chip - 1, c_half(near, i), i)

    def block_part(p, j):
        start = pl.multiple_of(j * rows, rows)
        return dot_nn(slab[p, :, pl.ds(start, rows)], c_block(j)[...])

    @pl.loop(0, aux)
    def _(p):
        acc[p] = acc[p] + block_part(p, near)

    for i in range(2):
        from_sib(OF_C, n_chip - 1, c_half(far, i), i)

    def end_half(p):
        h_own[p] = (acc[p] + block_part(p, far)).astype(BF16)

    def h_slot(c, a, i):
        return h_buf.at[c * aux + a * half_aux + i]

    def upper(s):
        top = 1 << (s.bit_length() - 1)
        return lax.rem(lax.div(chip, top), 2)

    def aux_from(s, i):
        if not two_hop:
            return half_aux * upper(s) + i
        ahead = 1 - bit1 if s > 1 else bit1
        if s == 3:
            return 2 * (parity if i == 0 else 1 - parity) + ahead
        return 2 * (1 - parity if s == 1 else parity) + (ahead if i == 0 else 1 - ahead)

    def aux_to(s, i):
        return 2 * (parity if s == 1 else 1 - parity) + (bit1 if i == 0 else 1 - bit1)

    if two_hop:
        for s, i in ((1, 0), (2, 0), (1, 1), (2, 1)):
            end_half(aux_to(s, i))
            to_chip(OF_H, s, h_own.at[aux_to(s, i)], h_slot(chip, core, i), i)
    else:
        pl.loop(0, aux)(end_half)
        for s in steps:
            for i in range(half_aux):
                to_chip(OF_H, s, h_own.at[half_aux * (1 - upper(s)) + i], h_slot(chip, core, i), i)
    own_slot = h_buf.at[pl.ds(chip * aux, aux)]
    send(h_own, own_slot, fwd_s.at[OF_H, 0, 0], fwd_r.at[OF_H, 0, 0], (z, sib))

    def pair(own_first, other, other_first, count):
        def add(p, total):
            return total + dot_nt(h_own[own_first + p], other[other_first + p])

        return lax.fori_loop(0, count, add, jnp.zeros((rows, rows), F32))

    k_block(b)[...] = pair(0, h_own, 0, aux)

    for s in range(1, n_grp):
        arrived(s_rows.at[flipped(z, s)], sz_s.at[s], sz_r.at[s])
    mid[:rows] = jnp.zeros((rows, mid.shape[1]), F32)

    @pl.loop(0, n_grp)
    def _(g):
        start = pl.multiple_of(g * width, width)
        mid[:rows] += dot_nn(s_rows[g], c_all[pl.ds(start, width), :])

    m_rows = (mid[:rows] * env_ref[...].astype(F32)).astype(BF16)

    @pl.loop(0, n_blk)
    def _(j):
        t_row(j)[...] = dot_nt(m_rows, c_block(j)[...]).astype(BF16)

    from_sib(OF_H, 0, own_slot)
    k_block(sib)[...] = pair(0, h_buf, chip * aux, aux)

    def sum_copy(c):
        return remote(k_send(c), k_recv.at[z], sum_s.at[c], sum_r.at[z], (c, b))

    line = n_grp == 4 and n_chip == 4
    adder = (z == 1) | (z == 2)
    far_end = n_grp - 1 - z if not line else jnp.where(z == 1, 3, 0)

    def is_far(c):
        return (c - z == 3) | (z - c == 3)

    def far_copy(c):
        return remote(k_send(c), k_far, far_s, far_r, (jnp.where(z == 0, 1, 2), b))

    def chunk_part(c, a):
        return slab.at[3, :, pl.ds(pl.multiple_of(c * width + a * rows, rows), rows)]

    def finish_chunk(c):
        @pl.when(jnp.logical_not(adder & (c == far_end)) if line else c >= 0)
        def _():
            for a in range(2):
                chunk_part(c, a)[...] = k_block(2 * c + a)[...].astype(BF16)
            if line:
                pl.when(is_far(c))(lambda: far_copy(c).start())
            near = (c != z) & jnp.logical_not(is_far(c)) if line else c != z
            pl.when(near)(lambda: sum_copy(c).start())

    def add_far():
        arrived(k_far, far_s, far_r)
        for a in range(2):
            part = k_block(2 * far_end + a)[...] + k_far[:, a * rows : (a + 1) * rows].astype(F32)
            chunk_part(far_end, a)[...] = part.astype(BF16)
        sum_copy(far_end).start()

    finish_chunk(chip)

    def exchange_block(s, a):
        c = flipped(chip, s)
        other = 2 * c + a
        block = sum(dot_nt(h_own[aux_from(s, i)], h_slot(c, a, i)[...]) for i in range(half_aux))
        k_block(other)[...] = block
        zt_send[other] = block.T.astype(BF16)
        send(zt_send.at[other], zt_recv.at[b], zt_s.at[2 * s + a], zt_r.at[2 * s + core], (z, other))

    def add_block(s):
        c = flipped(chip, s)
        for a in range(2):
            other = 2 * c + a
            arrived(zt_recv.at[other], zt_s.at[2 * s + a], zt_r.at[2 * s + a])
            k_block(other)[...] += zt_recv[other].astype(F32)
        finish_chunk(c)

    def h_arrives(s, i):
        slot = h_slot(flipped(chip, s), core, i)
        from_chip(OF_H, s, slot, i)
        to_sib(OF_H, s, slot, i)

    def exchange_step(s):
        exchange_block(s, core)
        for i in range(half_aux):
            from_sib(OF_H, s, h_slot(flipped(chip, s), 1 - core, i), i)
        exchange_block(s, 1 - core)

    if two_hop:
        for s, i in ((1, 0), (2, 0), (1, 1), (2, 1)):
            h_arrives(s, i)
        for s in (1, 2):
            c = flipped(chip, s)
            to_chip(OF_H, 3, h_slot(c, core, 0), h_slot(c, core, s - 1), s - 1, via=3 - s)
        exchange_step(1)
        exchange_step(2)
        add_block(1)
        add_block(2)
        h_arrives(3, 0)
        h_arrives(3, 1)
        exchange_step(3)
    else:
        for s in steps:
            for i in range(half_aux):
                h_arrives(s, i)
            exchange_step(s)
            if s > 1:
                add_block(s - 1)
    if line:
        pl.when(adder & (far_end != flipped(chip, n_chip - 1)))(add_far)
    add_block(n_chip - 1)
    if line:
        pl.when(adder & (far_end == flipped(chip, n_chip - 1)))(add_far)
    to_sib(OF_S, 0, s_cols.at[b])
    for s in steps:
        to_chip(OF_S, s, s_cols.at[b], s_cols.at[b])

    def add_margin(j):
        mid[...] += dot_tn(s_cols[j], c_block(j)[...])

    mid[...] = dot_tn(s_cols[b], c_block(b)[...])
    from_sib(OF_S, 0, s_cols.at[sib])
    add_margin(sib)
    for s in steps:
        other = 2 * flipped(chip, s)
        from_chip(OF_S, s, s_cols.at[other + core])
        to_sib(OF_S, s, s_cols.at[other + core])
        add_margin(other + core)
    for s in steps:
        other = 2 * flipped(chip, s) + 1 - core
        from_sib(OF_S, s, s_cols.at[other])
        add_margin(other)
    m_cols = (mid[...] * env_ref[...].astype(F32)).astype(BF16)

    out_ref[:, :rows] = k_block(2 * z)[...]
    out_ref[:, rows:] = k_block(2 * z + 1)[...]

    def add_sum(other):
        arrived(k_recv.at[other], sum_s.at[other], sum_r.at[other])
        out_ref[...] += k_recv[other].astype(F32)

    for s in range(1, n_grp):
        if line and s == 3:
            pl.when(adder)(lambda: add_sum(flipped(z, 3)))
        else:
            add_sum(flipped(z, s))
    k_bf = out_ref[...].astype(BF16)
    k_cols[b] = k_bf
    k_rows[z] = k_bf
    def row_copy(g, sems, to):
        return remote(k_rows.at[g], k_rows.at[g], sems.at[g], kz_r.at[g], (to, b))

    def pass_rows(g, ahead, wait):
        def act(copy):
            copy.wait_send() if wait else copy.start()

        if ahead > 0:
            pl.when(z < n_grp - 1)(lambda: act(row_copy(g, kz_up, z + 1)))
        else:
            pl.when(z > 0)(lambda: act(row_copy(g, kz_down, z - 1)))

    if line:
        pass_rows(z, 1, False)
        pass_rows(z, -1, False)
    else:
        for s in range(1, n_grp):
            send(k_rows.at[z], k_rows.at[z], kz_up.at[s], kz_r.at[s], (flipped(z, s), b))
    to_sib(OF_K, 0, k_cols.at[b])
    for s in steps:
        to_chip(OF_K, s, k_cols.at[b], k_cols.at[b])

    @pl.loop(0, n_blk)
    def _(j):
        t_col(j)[...] = dot_nt(c_block(j)[...], m_cols).astype(BF16)

    def take_first(j):
        out_ref[...] -= dot_nn(t_row(j)[...], k_cols[j])

    def take_second(g):
        out_ref[...] -= dot_nn(k_rows[g, :, :rows], t_col(2 * g)[...])
        out_ref[...] -= dot_nn(k_rows[g, :, rows:], t_col(2 * g + 1)[...])

    def line_rows(d, wait=False):
        for ahead in (1, -1):
            g = z - ahead * d

            @pl.when(z >= d if ahead > 0 else z < n_grp - d)
            def _():
                if not wait:
                    arrived(k_rows.at[g], kz_up.at[g], kz_r.at[g])
                pass_rows(g, ahead, wait)
                if not wait:
                    take_second(g)

    def cols_arrive(s):
        other = 2 * flipped(chip, s) + core
        from_chip(OF_K, s, k_cols.at[other])
        to_sib(OF_K, s, k_cols.at[other])
        take_first(other)

    take_first(b)
    take_second(z)
    from_sib(OF_K, 0, k_cols.at[sib])
    take_first(sib)
    if line:
        line_rows(1)
    for s in steps:
        cols_arrive(s)
        if line and s == 1:
            line_rows(2)
    for s in steps:
        other = 2 * flipped(chip, s) + 1 - core
        from_sib(OF_K, s, k_cols.at[other])
        take_first(other)
    if line:
        line_rows(3)
        pass_rows(z, 1, True)
        pass_rows(z, -1, True)
        line_rows(1, True)
        line_rows(2, True)
        line_rows(3, True)
    else:
        for s in range(1, n_grp):
            other = flipped(z, s)
            arrived(k_rows.at[other], kz_up.at[s], kz_r.at[s])
            take_second(other)

    for copy in sent:
        copy.wait_send()
    for s in range(n_chip):
        c = flipped(chip, s)

        if line:
            pl.when(is_far(c))(lambda: far_copy(c).wait_send())
        near = (c != z) & jnp.logical_not(is_far(c)) if line else c != z
        pl.when(near)(lambda: sum_copy(c).wait_send())


def on_device(n_grp, n_blk, slab, block_mask, orbitals, margin, env_flag):
    aux, rows, nao = slab.shape
    occ = orbitals.shape[1]
    width = margin.shape[1]
    n_chip = n_blk // 2
    assert width == 2 * rows and n_chip == n_grp and aux == 4
    env = env_flag[None, :]
    vmem = pl.BlockSpec(memory_space=pltpu.VMEM)
    dma = pltpu.SemaphoreType.DMA
    return pl.pallas_call(
        functools.partial(kernel, n_grp, n_blk),
        out_shape=jax.ShapeDtypeStruct((rows, width), F32),
        in_specs=[vmem] * 4 + [pl.BlockSpec(memory_space=pl.ANY)],
        out_specs=vmem,
        scratch_shapes=[
            pltpu.VMEM((aux, rows, nao), BF16),
            pltpu.VMEM((nao, occ), BF16),
            pltpu.VMEM((aux, rows, occ), F32),
            pltpu.VMEM((aux, rows, occ), BF16),
            pltpu.VMEM((n_chip * aux, rows, occ), BF16),
            pltpu.VMEM((n_blk, rows, rows), BF16),
            pltpu.VMEM((n_blk, rows, rows), BF16),
            pltpu.VMEM((n_grp, rows, width), BF16),
            pltpu.VMEM((n_blk, rows, width), BF16),
            pltpu.VMEM((n_grp, rows, width), BF16),
            pltpu.VMEM((n_blk, rows, width), BF16),
            pltpu.VMEM((n_grp, rows, width), BF16),
            pltpu.VMEM((width, occ), F32),
            pltpu.VMEM((rows, width), BF16),
            dma(()),
            dma((4, n_chip, 2)), dma((4, n_chip, 2)), dma((4, n_chip, 2)), dma((4, n_chip, 2)),
            dma((2 * n_chip,)), dma((2 * n_chip,)),
            dma((n_grp,)), dma((n_grp,)), dma((n_grp,)), dma((n_grp,)), dma((n_grp,)), dma((n_grp,)),
            dma((n_grp,)), dma(()), dma(()),
        ],
        compiler_params=pltpu.CompilerParams(
            collective_id=0, has_side_effects=True, vmem_limit_bytes=63 * 2**20
        ),
    )(block_mask, env, orbitals, margin, slab)


def solution(mesh):
    placed = (P("grp", "blk", None), P("grp", "blk", None), P("blk", None), P("blk", "grp"), P())
    return jax.shard_map(
        functools.partial(on_device, mesh.shape["grp"], mesh.shape["blk"]),
        mesh=mesh, in_specs=placed, out_specs=P("blk", "grp"), check_vma=False,
    )
```

```python
import functools

import jax
import jax.numpy as jnp
from jax import lax
from jax.experimental import pallas as pl
from jax.experimental.pallas import tpu as pltpu
from jax.sharding import PartitionSpec as P

ATILE = 32
MESH = pl.DeviceIdType.MESH
BF16 = jnp.bfloat16
F32 = jnp.float32
OF_C, OF_H, OF_K, OF_S = range(4)


def dot_nn(left, right):
    return lax.dot_general(left, right, (((1,), (0,)), ((), ())), preferred_element_type=F32)


def dot_nt(left, right):
    return lax.dot_general(left, right, (((1,), (1,)), ((), ())), preferred_element_type=F32)


def dot_tn(left, right):
    return lax.dot_general(left, right, (((0,), (0,)), ((), ())), preferred_element_type=F32)


def flipped(index, step):
    bit = 1
    while bit <= step:
        if step & bit:
            index = index + bit - 2 * bit * lax.rem(lax.div(index, bit), 2)
        bit *= 2
    return index


def kernel(
    n_grp, n_blk,
    mask_ref, env_ref, orb_ref, margin_ref, slab_hbm, out_ref,
    slab, c_all, acc, h_own, h_buf, zt_send, zt_recv, k_recv,
    k_cols, k_rows, s_cols, s_rows, mid,
    load_sem, dir_s, dir_r, fwd_s, fwd_r, zt_s, zt_r, sum_s, sum_r, kz_s, kz_r, sz_s, sz_r,
):
    z = lax.axis_index("grp")
    b = lax.axis_index("blk")
    n_chip = n_blk // 2
    chip, core = lax.div(b, 2), lax.rem(b, 2)
    sib = chip * 2 + 1 - core
    aux, rows, nao = slab.shape
    half_aux = aux // 2
    width = 2 * rows
    steps = range(1, n_chip)
    two_hop = n_chip == 4
    bit1 = lax.div(chip, 2)
    parity = lax.rem(lax.rem(chip, 2) + bit1, 2)
    sent = []

    load = pltpu.make_async_copy(slab_hbm, slab, load_sem)
    load.start()

    barrier = pltpu.get_barrier_semaphore()
    for s in range(1, n_blk):
        pl.semaphore_signal(barrier, inc=1, device_id=(z, lax.rem(b + s, n_blk)), device_id_type=MESH)
    for s in range(1, n_grp):
        pl.semaphore_signal(barrier, inc=1, device_id=(lax.rem(z + s, n_grp), b), device_id_type=MESH)
    pl.semaphore_wait(barrier, n_blk + n_grp - 2)

    def remote(src, dst, send_sem, recv_sem, to):
        return pltpu.make_async_remote_copy(
            src_ref=src, dst_ref=dst, send_sem=send_sem, recv_sem=recv_sem,
            device_id=to, device_id_type=MESH,
        )

    def send(src, dst, send_sem, recv_sem, to):
        copy = remote(src, dst, send_sem, recv_sem, to)
        copy.start()
        sent.append(copy)

    def arrived(dst, send_sem, recv_sem):
        remote(dst, dst, send_sem, recv_sem, (z, sib)).wait_recv()

    def to_chip(kind, s, src, dst, i=0, via=None):
        to = (z, flipped(chip, via or s) * 2 + core)
        send(src, dst, dir_s.at[kind, s, i], dir_r.at[kind, s, i], to)

    def from_chip(kind, s, dst, i=0):
        arrived(dst, dir_s.at[kind, s, i], dir_r.at[kind, s, i])

    def to_sib(kind, s, ref, i=0):
        send(ref, ref, fwd_s.at[kind, s, i], fwd_r.at[kind, s, i], (z, sib))

    def from_sib(kind, s, dst, i=0):
        arrived(dst, fwd_s.at[kind, s, i], fwd_r.at[kind, s, i])

    per_acc = acc.shape[2] // rows

    def k_block(j):
        start = pl.multiple_of(lax.rem(j, per_acc) * rows, rows)
        return acc.at[lax.div(j, per_acc), :, pl.ds(start, rows)]

    def t_row(j):
        return slab.at[2, :, pl.ds(pl.multiple_of(j * rows, rows), rows)]

    def t_col(j):
        start = pl.multiple_of(lax.rem(j, n_grp) * width, width)
        return slab.at[lax.div(j, n_grp), :, pl.ds(start, width)]

    def k_send(c):
        return slab.at[3, :, pl.ds(pl.multiple_of(c * width, width), width)]

    def c_block(index):
        return c_all.at[pl.ds(pl.multiple_of(index * rows, rows), rows)]

    c_block(b)[...] = orb_ref[...]
    to_sib(OF_C, 0, c_block(b))

    def c_half(index, i):
        start = pl.multiple_of(index * rows + i * (rows // 2), rows // 2)
        return c_all.at[pl.ds(start, rows // 2)]

    if two_hop:
        for s, i in ((1, 0), (2, 1), (1, 1), (2, 0)):
            to_chip(OF_C, s, c_half(b, i), c_half(b, i), i)
    else:
        for s in steps:
            for i in range(2):
                to_chip(OF_C, s, c_half(b, i), c_half(b, i), i)
    s_rows[z] = margin_ref[...]
    s_cols[b] = margin_ref[...]
    for s in range(1, n_grp):
        send(s_rows.at[z], s_rows.at[z], sz_s.at[s], sz_r.at[s], (flipped(z, s), b))

    spread = lax.broadcasted_iota(jnp.int32, (nao // ATILE, nao), 1)
    tile = lax.broadcasted_iota(jnp.int32, (nao // ATILE, nao), 0) * ATILE
    spread = jnp.where((spread >= tile) & (spread < tile + ATILE), 1.0, 0.0).astype(BF16)
    keep_all = dot_nn(mask_ref[0].astype(F32).astype(BF16), spread)
    load.wait()
    for t in range(rows // ATILE):
        keep = jnp.broadcast_to(keep_all[t : t + 1, :], (ATILE, nao)).astype(BF16)

        @pl.loop(0, aux)
        def _(p):
            slab[p, t * ATILE : (t + 1) * ATILE, :] = slab[p, t * ATILE : (t + 1) * ATILE, :] * keep

    def half_part(p, c):
        start = pl.multiple_of(c * width, width)
        return dot_nn(slab[p, :, pl.ds(start, width)], c_all[pl.ds(start, width), :])

    from_sib(OF_C, 0, c_block(sib))

    def start_half(c, first):
        @pl.loop(0, aux)
        def _(p):
            part = half_part(p, c)
            acc[p] = part if first else acc[p] + part

    def c_arrives(s, i):
        from_chip(OF_C, s, c_half(flipped(chip, s) * 2 + core, i), i)

    def c_crosses(s):
        to_sib(OF_C, s, c_block(flipped(chip, s) * 2 + core))

    if two_hop:
        for s, i in ((1, 0), (2, 1)):
            c_arrives(s, i)
            part = c_half(flipped(chip, s) * 2 + core, i)
            to_chip(OF_C, 3, part, part, i, via=3 - s)
    start_half(chip, True)
    if two_hop:
        c_arrives(1, 1)
        c_crosses(1)
        c_arrives(2, 0)
        c_crosses(2)
    else:
        for s in steps[:-1]:
            c_arrives(s, 0)
            c_arrives(s, 1)
            c_crosses(s)
    for s in steps[:-1]:
        from_sib(OF_C, s, c_block(flipped(chip, s) * 2 + 1 - core))
        start_half(flipped(chip, s), False)
    c_last = flipped(chip, n_chip - 1)
    c_arrives(n_chip - 1, 0)
    c_arrives(n_chip - 1, 1)
    c_crosses(n_chip - 1)
    from_sib(OF_C, n_chip - 1, c_block(c_last * 2 + 1 - core))

    def end_half(p):
        h_own[p] = (acc[p] + half_part(p, c_last)).astype(BF16)

    def h_slot(c, a, i):
        return h_buf.at[c * aux + a * half_aux + i]

    def upper(s):
        top = 1 << (s.bit_length() - 1)
        return lax.rem(lax.div(chip, top), 2)

    def aux_from(s, i):
        if not two_hop:
            return half_aux * upper(s) + i
        ahead = 1 - bit1 if s > 1 else bit1
        if s == 3:
            return 2 * (parity if i == 0 else 1 - parity) + ahead
        return 2 * (1 - parity if s == 1 else parity) + (ahead if i == 0 else 1 - ahead)

    if two_hop:
        for s, i in ((1, 0), (2, 0), (1, 1), (2, 1)):
            p = 2 * (parity if s == 1 else 1 - parity) + (bit1 if i == 0 else 1 - bit1)
            end_half(p)
            to_chip(OF_H, s, h_own.at[p], h_slot(chip, core, i), i)
    else:
        pl.loop(0, aux)(end_half)
        for s in steps:
            for i in range(half_aux):
                to_chip(OF_H, s, h_own.at[half_aux * (1 - upper(s)) + i], h_slot(chip, core, i), i)
    own_slot = h_buf.at[pl.ds(chip * aux, aux)]
    send(h_own, own_slot, fwd_s.at[OF_H, 0, 0], fwd_r.at[OF_H, 0, 0], (z, sib))

    def pair(own_first, other, other_first, count):
        def add(p, total):
            return total + dot_nt(h_own[own_first + p], other[other_first + p])

        return lax.fori_loop(0, count, add, jnp.zeros((rows, rows), F32))

    k_block(b)[...] = pair(0, h_own, 0, aux)

    for s in range(1, n_grp):
        arrived(s_rows.at[flipped(z, s)], sz_s.at[s], sz_r.at[s])
    mid[:rows] = jnp.zeros((rows, mid.shape[1]), F32)

    @pl.loop(0, n_grp)
    def _(g):
        start = pl.multiple_of(g * width, width)
        mid[:rows] += dot_nn(s_rows[g], c_all[pl.ds(start, width), :])

    m_rows = (mid[:rows] * env_ref[...].astype(F32)).astype(BF16)

    @pl.loop(0, n_blk)
    def _(j):
        t_row(j)[...] = dot_nt(m_rows, c_block(j)[...]).astype(BF16)

    from_sib(OF_H, 0, own_slot)
    k_block(sib)[...] = pair(0, h_buf, chip * aux, aux)

    def sum_copy(c):
        return remote(k_send(c), k_recv.at[z], sum_s.at[c], sum_r.at[z], (c, b))

    def finish_chunk(c):
        for a in range(2):
            at = pl.multiple_of(c * width + a * rows, rows)
            slab[3, :, pl.ds(at, rows)] = k_block(2 * c + a)[...].astype(BF16)

        @pl.when(c != z)
        def _():
            sum_copy(c).start()

    finish_chunk(chip)

    def exchange_block(s, a):
        c = flipped(chip, s)
        other = 2 * c + a
        block = sum(dot_nt(h_own[aux_from(s, i)], h_slot(c, a, i)[...]) for i in range(half_aux))
        k_block(other)[...] = block
        zt_send[other] = block.T.astype(BF16)
        send(zt_send.at[other], zt_recv.at[b], zt_s.at[2 * s + a], zt_r.at[2 * s + core], (z, other))

    def add_block(s):
        c = flipped(chip, s)
        for a in range(2):
            other = 2 * c + a
            arrived(zt_recv.at[other], zt_s.at[2 * s + a], zt_r.at[2 * s + a])
            k_block(other)[...] += zt_recv[other].astype(F32)
        finish_chunk(c)

    def h_arrives(s, i):
        slot = h_slot(flipped(chip, s), core, i)
        from_chip(OF_H, s, slot, i)
        to_sib(OF_H, s, slot, i)

    def exchange_step(s):
        exchange_block(s, core)
        for i in range(half_aux):
            from_sib(OF_H, s, h_slot(flipped(chip, s), 1 - core, i), i)
        exchange_block(s, 1 - core)

    if two_hop:
        for s, i in ((1, 0), (2, 0), (1, 1), (2, 1)):
            h_arrives(s, i)
        for s in (1, 2):
            c = flipped(chip, s)
            to_chip(OF_H, 3, h_slot(c, core, 0), h_slot(c, core, s - 1), s - 1, via=3 - s)
        exchange_step(1)
        exchange_step(2)
        add_block(1)
        add_block(2)
        h_arrives(3, 0)
        h_arrives(3, 1)
        exchange_step(3)
    else:
        for s in steps:
            for i in range(half_aux):
                h_arrives(s, i)
            exchange_step(s)
            if s > 1:
                add_block(s - 1)
    add_block(n_chip - 1)
    to_sib(OF_S, 0, s_cols.at[b])
    for s in steps:
        to_chip(OF_S, s, s_cols.at[b], s_cols.at[b])

    def tile_copies():
        copies = []
        for s in range(1, n_grp):
            to = (flipped(z, s), b)
            copies.append(remote(k_rows.at[z], k_rows.at[z], kz_s.at[s], kz_r.at[s], to))
        mine = k_cols.at[b]
        copies.append(remote(mine, mine, fwd_s.at[OF_K, 0, 0], fwd_r.at[OF_K, 0, 0], (z, sib)))
        for s in steps:
            to = (z, flipped(chip, s) * 2 + core)
            copies.append(remote(mine, mine, dir_s.at[OF_K, s, 0], dir_r.at[OF_K, s, 0], to))
        return copies

    def finish_tile():
        out_ref[:, :rows] = k_block(2 * z)[...]
        out_ref[:, rows:] = k_block(2 * z + 1)[...]
        for s in range(1, n_grp):
            other = flipped(z, s)
            arrived(k_recv.at[other], sum_s.at[other], sum_r.at[other])
            out_ref[...] += k_recv[other].astype(F32)
        k_bf = out_ref[...].astype(BF16)
        k_cols[b] = k_bf
        k_rows[z] = k_bf
        for copy in tile_copies():
            copy.start()

    last = flipped(chip, n_chip - 1)
    pl.when(z != last)(finish_tile)

    def add_margin(j):
        mid[...] += dot_tn(s_cols[j], c_block(j)[...])

    mid[...] = dot_tn(s_cols[b], c_block(b)[...])
    from_sib(OF_S, 0, s_cols.at[sib])
    add_margin(sib)
    for s in steps:
        other = 2 * flipped(chip, s)
        from_chip(OF_S, s, s_cols.at[other + core])
        to_sib(OF_S, s, s_cols.at[other + core])
        add_margin(other + core)
    for s in steps:
        other = 2 * flipped(chip, s) + 1 - core
        from_sib(OF_S, s, s_cols.at[other])
        add_margin(other)
    m_cols = (mid[...] * env_ref[...].astype(F32)).astype(BF16)

    pl.when(z == last)(finish_tile)

    @pl.loop(0, n_blk)
    def _(j):
        t_col(j)[...] = dot_nt(c_block(j)[...], m_cols).astype(BF16)

    def take_first(j):
        out_ref[...] -= dot_nn(t_row(j)[...], k_cols[j])

    def take_second(g):
        out_ref[...] -= dot_nn(k_rows[g, :, :rows], t_col(2 * g)[...])
        out_ref[...] -= dot_nn(k_rows[g, :, rows:], t_col(2 * g + 1)[...])

    def cols_arrive(s):
        other = 2 * flipped(chip, s) + core
        from_chip(OF_K, s, k_cols.at[other])
        to_sib(OF_K, s, k_cols.at[other])
        take_first(other)

    take_first(b)
    take_second(z)
    from_sib(OF_K, 0, k_cols.at[sib])
    take_first(sib)
    for s in steps:
        cols_arrive(s)
    for s in steps:
        other = 2 * flipped(chip, s) + 1 - core
        from_sib(OF_K, s, k_cols.at[other])
        take_first(other)
    for s in range(1, n_grp):
        other = flipped(z, s)
        arrived(k_rows.at[other], kz_s.at[s], kz_r.at[s])
        take_second(other)

    for copy in tile_copies():
        copy.wait_send()
    for copy in sent:
        copy.wait_send()
    for s in range(n_chip):
        c = flipped(chip, s)

        @pl.when(c != z)
        def _():
            sum_copy(c).wait_send()


def on_device(n_grp, n_blk, slab, block_mask, orbitals, margin, env_flag):
    aux, rows, nao = slab.shape
    occ = orbitals.shape[1]
    width = margin.shape[1]
    n_chip = n_blk // 2
    assert width == 2 * rows and n_chip == n_grp and aux == 4
    env = env_flag[None, :]
    vmem = pl.BlockSpec(memory_space=pltpu.VMEM)
    dma = pltpu.SemaphoreType.DMA
    return pl.pallas_call(
        functools.partial(kernel, n_grp, n_blk),
        out_shape=jax.ShapeDtypeStruct((rows, width), F32),
        in_specs=[vmem] * 4 + [pl.BlockSpec(memory_space=pl.ANY)],
        out_specs=vmem,
        scratch_shapes=[
            pltpu.VMEM((aux, rows, nao), BF16),
            pltpu.VMEM((nao, occ), BF16),
            pltpu.VMEM((aux, rows, occ), F32),
            pltpu.VMEM((aux, rows, occ), BF16),
            pltpu.VMEM((n_chip * aux, rows, occ), BF16),
            pltpu.VMEM((n_blk, rows, rows), BF16),
            pltpu.VMEM((n_blk, rows, rows), BF16),
            pltpu.VMEM((n_grp, rows, width), BF16),
            pltpu.VMEM((n_blk, rows, width), BF16),
            pltpu.VMEM((n_grp, rows, width), BF16),
            pltpu.VMEM((n_blk, rows, width), BF16),
            pltpu.VMEM((n_grp, rows, width), BF16),
            pltpu.VMEM((width, occ), F32),
            dma(()),
            dma((4, n_chip, 2)), dma((4, n_chip, 2)), dma((4, n_chip, 2)), dma((4, n_chip, 2)),
            dma((2 * n_chip,)), dma((2 * n_chip,)),
            dma((n_grp,)), dma((n_grp,)), dma((n_grp,)), dma((n_grp,)), dma((n_grp,)), dma((n_grp,)),
        ],
        compiler_params=pltpu.CompilerParams(
            collective_id=0, has_side_effects=True, vmem_limit_bytes=63 * 2**20
        ),
    )(block_mask, env, orbitals, margin, slab)


def solution(mesh):
    placed = (P("grp", "blk", None), P("grp", "blk", None), P("blk", None), P("blk", "grp"), P())
    return jax.shard_map(
        functools.partial(on_device, mesh.shape["grp"], mesh.shape["blk"]),
        mesh=mesh, in_specs=placed, out_specs=P("blk", "grp"), check_vma=False,
    )
```
